256 devices in a mesh: pp: 8 (over y, z_hi), ep: 32 (over x, z_lo, core).
Axes of the slice: x: 4, y: 4, z: 8 (z_hi: 2, z_lo: 4; z = z_hi * 4 + z_lo), core: 2. Of those that a mesh axis runs over, the one named last changes fastest.
Arguments:
- out_grads: bfloat16 [8, 4096, 3584], P('pp', 'ep'), may hold values from -6 to 6
- expert_ids: int32 [8, 4096, 8], P('pp', 'ep'), may hold values from 0 to 31, all different within a row; in each aligned block of 128 rows (0 to 127, 128 to 255, ..., all dimensions but the last counted through in order) at most 48 rows name the same one
- router_logits: float32 [8, 4096, 32], P('pp', 'ep'), may hold values from -6 to 6
- hidden_acts: bfloat16 [8, 32, 1536, 1024], P('pp', 'ep'), may hold values from -6 to 6
- w_down: bfloat16 [8, 32, 1024, 3584], P('pp', 'ep'), may hold values from -0.1875 to 0.1875
- w_router: bfloat16 [8, 32, 3584], P('pp'), may hold values from -0.59765625 to 0.59765625
Outputs:
- incoming: bfloat16 [8, 4096, 3584], P('pp', 'ep')
The draws below stay inside these ranges and needn't reach their ends.
Inputs may be any that keep to these rules, and one draw needn't show every extreme that they name: `expert_ids`: each row names 8 different experts; among the 128 tokens of one device for one section no expert is named more than 48 times, a bound that some block reaches.
All inputs are finite; a program needn't handle non-finite values.
Results may differ from the reference program's by a relative error of at most 0.0049.
Values may be sent and summed in bfloat16 or wider, within the bound.
A program may use at most 128 MiB of HBM per device.

```python
import math
import jax
import jax.numpy as jnp
import numpy as np
from jax import lax

D = 3584
FFW = 1024
TOP = 8
TOK = 128
EXPERTS = 32
MOST = 48
SLOTS = 1536
TOKENS = 4096
N_PP = 8
N_EP = 32


def levels(stream_key, shape, pieces, low, top_value):
    factor_of = 1.0
    for position, blocks in pieces:
        draws = jax.random.uniform(jax.random.fold_in(jax.random.fold_in(stream_key, 6), position), (blocks,), jnp.float32, low / len(pieces), top_value / len(pieces))
        factor_of = factor_of * jnp.repeat(jnp.exp(draws), shape[position] // blocks).reshape((-1,) + (1,) * (len(shape) - 1 - position))
    return factor_of


def assign_block(rng, own, number, rows, amount, top, most, lean):
    sequence = jax.random.permutation(rng, amount)
    crowded, ordinary = load_shares(amount, rows * top, most, lean, True), load_shares(amount, rows * top, most, lean, False)
    places = jnp.arange(amount)

    def named(sizes, offset_by):
        used = int((sizes > 0).sum())
        fixed = max(1, used // 4)
        moved = fixed + (places - fixed + offset_by * (used - fixed)) % max(1, amount - fixed)
        return jnp.zeros((amount,), jnp.int32).at[sequence[jnp.where(places < fixed, places, moved)]].set(jnp.asarray(sizes, jnp.int32))

    sizes = jnp.where(number % 4 == 0, named(crowded, number // 4), named(ordinary, number - number // 4 - 1))
    mixed = jax.random.permutation(jax.random.fold_in(own, 3), amount)
    giver, sink = mixed[0:amount // 2 * 2:2], mixed[1:amount // 2 * 2:2]
    margin = jnp.minimum(sizes[giver] - 1, most - sizes[sink]) // 2
    margin = jnp.where((giver == sequence[0]) | (sink == sequence[0]) | (sizes[sink] == 0), 0, jnp.maximum(margin, 0))
    moved = jax.random.randint(jax.random.fold_in(own, 4), (amount // 2,), 0, 1 << 20) % (margin + 1)
    sizes = sizes.at[giver].add(-moved).at[sink].add(moved)
    items = jnp.searchsorted(jnp.cumsum(sizes), jnp.arange(rows * top), side="right").astype(jnp.int32)
    table = items.reshape(top, rows).T
    table = table[jax.random.permutation(jax.random.fold_in(own, 1), rows)]
    offset_by = jax.random.randint(jax.random.fold_in(own, 2), (rows, 1), 0, top)
    return jnp.take_along_axis(table, (jnp.arange(top)[None, :] + offset_by) % top, axis=1)


def load_shares(number_of, total, most, slope, full):
    loads = [(1 << 20) // math.isqrt(grade ** slope) + 1 for grade in range(1, number_of + 1)]
    largest = most if full else min(most, max(-(-total // number_of), total * loads[0] // sum(loads)))
    least = 1 if total - largest >= number_of - 1 else 0
    given, rest = [largest] + [least] * (number_of - 1), total - largest - least * (number_of - 1)
    while rest > 0:
        candidates = [i for i in range(1, number_of) if given[i] < largest] or [i for i in range(1, number_of) if given[i] < most]
        pool, budget = sum([loads[i] for i in candidates]), rest
        for i in candidates:
            more = min(most - given[i], max(1, budget * loads[i] // pool), rest)
            given[i] = given[i] + more
            rest = rest - more
    return np.array(given)


def normal_values(own_key, extent, scale, most, pieces=(), kind=jnp.bfloat16):
    drawn = scale * jax.random.normal(own_key, extent, jnp.float32)
    if pieces:
        drawn = drawn * levels(own_key, extent, pieces, -0.22, 0.18)
    return jnp.clip(drawn, -most, most).astype(kind)


def setup_inputs(seed: int = 0) -> dict:
    keys = jax.random.split(jax.random.key(seed), 7)
    out_grads = normal_values(keys[0], (N_PP, TOKENS, D), 1.0, 6.0, ((0, 8), (1, 32)))
    expert_ids_keys = jax.random.split(jax.random.fold_in(keys[1], 1), N_PP * TOKENS // TOK)
    expert_ids_turns = jax.random.permutation(jax.random.fold_in(keys[1], 3), N_PP * TOKENS // TOK)
    expert_ids = jax.vmap(lambda own, number: assign_block(jax.random.fold_in(keys[1], 2), own, number, TOK, EXPERTS, TOP, MOST, 2))(expert_ids_keys, expert_ids_turns).reshape((N_PP, TOKENS, TOP))
    router_logits = normal_values(keys[2], (N_PP, TOKENS, EXPERTS), 1.5, 6.0, ((0, 8), (1, 32)), jnp.float32)
    hidden_acts = normal_values(keys[3], (N_PP, EXPERTS, SLOTS, FFW), 1.0, 6.0, ((0, 8), (1, 32)))
    w_down = normal_values(keys[4], (N_PP, EXPERTS, FFW, D), FFW ** -0.5, 0.1875, ((0, 8), (1, 32)))
    w_router = normal_values(keys[5], (N_PP, EXPERTS, D), 0.1, 0.59765625, ((0, 8),))
    return dict(out_grads=out_grads, expert_ids=expert_ids, router_logits=router_logits, hidden_acts=hidden_acts, w_down=w_down, w_router=w_router)


def slot_ranks(chosen, num_experts):
    flat_ids = chosen.reshape(-1)
    onehot = (flat_ids[:, None] == jnp.arange(num_experts, dtype=jnp.int32)[None, :]).astype(jnp.int32)
    before = jnp.cumsum(onehot, axis=0) - onehot
    return lax.optimization_barrier(jnp.sum(before * onehot, axis=1)).reshape(chosen.shape).astype(jnp.int32)

def router_grad(score_grad, chosen, logits, router_weight):
    num_experts = logits.shape[1]
    affinity = jax.nn.sigmoid(logits.astype(jnp.float32))
    picked = jnp.take_along_axis(affinity, chosen, axis=1)
    picked_sum = lax.optimization_barrier(jnp.sum(picked, axis=1, keepdims=True))
    weight = picked / picked_sum
    mean_grad = lax.optimization_barrier(jnp.sum(weight * score_grad, axis=1, keepdims=True))
    logit_grad = (score_grad - mean_grad) / picked_sum * picked * (1.0 - picked)
    marks = (chosen[:, :, None] == jnp.arange(num_experts, dtype=jnp.int32)[None, None, :]).astype(jnp.float32)
    logit_table = lax.optimization_barrier(jnp.sum(marks * logit_grad[:, :, None], axis=1)).astype(jnp.bfloat16)
    return jnp.dot(logit_table, router_weight, preferred_element_type=jnp.float32).astype(jnp.bfloat16)

def reference(out_grads, expert_ids, router_logits, hidden_acts, w_down, w_router):
    results = []
    for section_index in range(N_PP):
        chosen = expert_ids[section_index]
        places = jax.vmap(lambda block: slot_ranks(block, EXPERTS))(chosen.reshape(N_EP, TOK, TOP)).reshape(TOKENS, TOP)
        owner = (jnp.arange(TOKENS, dtype=jnp.int32) // TOK)[:, None]
        slots = (owner * MOST + places).astype(jnp.int32)
        token_index = jnp.broadcast_to(jnp.arange(TOKENS, dtype=jnp.int32)[:, None], (TOKENS, TOP))
        slot_table = jnp.zeros((EXPERTS, SLOTS), jnp.int32).at[chosen, slots].set(token_index)
        upstream = out_grads[section_index].astype(jnp.float32)

        def per_expert(expert_index):
            produced = jnp.dot(hidden_acts[section_index, expert_index].astype(jnp.float32), w_down[section_index, expert_index].astype(jnp.float32), preferred_element_type=jnp.float32)
            spread_rows = upstream[slot_table[expert_index]]
            return lax.optimization_barrier(jnp.sum(produced * spread_rows, axis=1))
        slot_scores = lax.map(per_expert, jnp.arange(EXPERTS, dtype=jnp.int32))
        score_grad = slot_scores[chosen, slots]
        results.append(router_grad(score_grad, chosen, router_logits[section_index], w_router[section_index]))
    all_grads = jnp.stack(results)
    blank_rows = jnp.zeros_like(all_grads[:1])
    return jnp.concatenate([all_grads[1:], blank_rows], axis=0)
```

```python
import jax
import jax.numpy as jnp
from jax import lax
from jax.sharding import PartitionSpec as P


def passed_along(x, axis, by):
    size = lax.axis_size(axis)
    pairs = [(i, i + by) for i in range(size) if 0 <= i + by < size]
    return lax.ppermute(x, axis, pairs)


def rank_table(chosen, num_experts):
    tokens = chosen.shape[0]
    hits = chosen[:, :, None] == jnp.arange(num_experts, dtype=jnp.int32)[None, None, :]
    named = jnp.any(hits, axis=1)
    earlier = jnp.tril(jnp.ones((tokens, tokens), jnp.bfloat16), -1)
    before = jnp.dot(earlier, named.astype(jnp.bfloat16), preferred_element_type=jnp.float32)
    return named, jnp.where(named, before, -1.0)


def on_device(out_grads, expert_ids, router_logits, hidden_acts, w_down, w_router):
    members = lax.axis_size("ep")
    num_experts = w_router.shape[1]
    chosen = expert_ids[0]
    named, ranks = rank_table(chosen, num_experts)
    upstream = lax.all_gather(out_grads[0], "ep", axis=0)
    rank_rows = lax.all_to_all(ranks.T, "ep", split_axis=0, concat_axis=0, tiled=True)
    next_router = passed_along(w_router[0], "pp", -1)
    activations = hidden_acts[0, 0]
    depth = activations.shape[0] // members
    produced = jnp.dot(
        activations, w_down[0, 0], preferred_element_type=jnp.float32
    ).astype(jnp.bfloat16)
    produced = produced.reshape(members, depth, -1)
    cross = lax.dot_general(
        upstream,
        produced,
        (((2,), (2,)), ((0,), (0,))),
        preferred_element_type=jnp.float32,
    )
    mask = rank_rows[:, :, None] == jnp.arange(depth, dtype=jnp.float32)[None, None, :]
    scores = jnp.sum(jnp.where(mask, cross, 0.0), axis=2)
    score_grad = lax.all_to_all(scores, "ep", split_axis=0, concat_axis=0, tiled=True).T
    picked = jnp.where(named, jax.nn.sigmoid(router_logits[0]), 0.0)
    picked_sum = jnp.sum(picked, axis=1, keepdims=True)
    mean_grad = jnp.sum(picked / picked_sum * score_grad, axis=1, keepdims=True)
    table = (score_grad - mean_grad) / picked_sum * picked * (1.0 - picked)
    table = passed_along(table.astype(jnp.bfloat16), "pp", -1)
    result = jnp.dot(table, next_router, preferred_element_type=jnp.float32)
    return result.astype(jnp.bfloat16)[None]


def solution(mesh):
    in_specs = (
        P("pp", "ep", None),
        P("pp", "ep", None),
        P("pp", "ep", None),
        P("pp", "ep", None, None),
        P("pp", "ep", None, None),
        P("pp", None, None),
    )
    out_specs = P("pp", "ep", None)
    return jax.shard_map(
        on_device, mesh=mesh, in_specs=in_specs, out_specs=out_specs, check_vma=False
    )
```

```python
import functools

import jax
import jax.numpy as jnp
from jax import lax
from jax.experimental import pallas as pl
from jax.experimental.pallas import tpu as pltpu
from jax.sharding import PartitionSpec as P

MESH = pl.DeviceIdType.MESH
F32, BF16 = jnp.float32, jnp.bfloat16

X, Z, CORES = 4, 4, 2
CHIPS = X * Z
TOK, D, FFW, MOST, EXPERTS = 128, 3584, 1024, 48, 32
WIDE, SLIM = 1408, 384
OFFSET = (0, WIDE, 2 * WIDE + SLIM, 2 * WIDE)
BULK = 2 * WIDE + SLIM
QUARTER = D // X
HALF = D // 2
RANK_ROWS = 16

ORDER = (
    (
        16, 48, 4, 17, 49, 5, 18, 50, 6, 19, 51, 7, 32, 20, 8, 21, 52, 9, 10, 22,
        54, 33, 53, 11, 34, 35, 23, 55, 24, 56, 12, 36, 25, 13, 14, 26, 37, 57, 58, 15,
        27, 59, 40, 28, 30, 62, 31, 41, 60, 63, 46, 47, 38, 29, 61, 39, 42, 43, 44, 45,
    ),
    (
        20, 52, 0, 8, 21, 53, 1, 9, 22, 54, 2, 10, 23, 55, 3, 11, 18, 50, 19, 36,
        16, 12, 51, 48, 24, 13, 14, 26, 58, 17, 56, 15, 27, 59, 34, 30, 35, 49, 25, 62,
        31, 63, 46, 37, 57, 47, 38, 39, 42, 43, 28, 60, 32, 29, 33, 61, 40, 41, 44, 45,
    ),
    (
        24, 56, 12, 4, 25, 57, 13, 5, 26, 58, 14, 6, 27, 59, 15, 7, 30, 62, 31, 40,
        20, 0, 63, 28, 52, 1, 2, 22, 54, 60, 21, 3, 23, 55, 46, 18, 47, 29, 53, 50,
        19, 51, 34, 41, 61, 35, 42, 43, 38, 39, 16, 48, 36, 17, 37, 49, 44, 45, 32, 33,
    ),
    (
        28, 60, 8, 29, 61, 9, 30, 62, 10, 31, 63, 11, 44, 24, 4, 25, 56, 5, 6, 26,
        58, 45, 57, 7, 46, 47, 27, 59, 20, 52, 0, 40, 21, 1, 2, 22, 41, 53, 54, 3,
        23, 55, 36, 16, 18, 50, 19, 37, 48, 51, 34, 35, 42, 17, 49, 43, 38, 39, 32, 33,
    ),
)
EARLY = 8


def programme(z):
    own = [4 * z + p for p in range(4)]
    late = own + list(ORDER[z][:EARLY])
    steps = []
    for code in ORDER[z][EARLY:]:
        if late:
            steps.append(late.pop(0))
        steps.append(code + 64)
    seen = {}
    out = []
    for code in steps:
        shard = code % 64 // 4
        seen[shard] = seen.get(shard, 0) + 1
        out.append(code + (128 if seen[shard] == 4 else 0))
    return tuple(out)


STEPS = tuple(programme(z) for z in range(Z))
COUNT = len(STEPS[0])


def packed(codes):
    words = []
    for k in range(0, len(codes), 3):
        words.append(sum(code << (8 * j) for j, code in enumerate(codes[k : k + 3])))
    return words


def by_row(z, values):
    picked = jnp.int32(values[Z - 1])
    for row in range(Z - 1):
        picked = jnp.where(z == row, jnp.int32(values[row]), picked)
    return picked


def entry(words, i):
    place = lax.div(i, 3)
    while len(words) > 1:
        odd = lax.rem(place, 2) == 1
        halved = []
        for k in range(0, len(words), 2):
            more = k + 1 < len(words)
            halved.append(jnp.where(odd, words[k + 1], words[k]) if more else words[k])
        words, place = halved, lax.div(place, 2)
    turn = lax.rem(i, 3)
    scale = jnp.where(turn == 0, 1, jnp.where(turn == 1, 1 << 8, 1 << 16))
    return lax.rem(lax.div(words[0], scale), 256)


def goes(way, x, z, xo, zo, piece):
    dx = lax.rem(xo - x + X, X)
    odd = lax.rem(piece, 2)
    slim = piece >= 2
    in_line = jnp.logical_or(slim, dx == 0)
    in_row = jnp.logical_or(jnp.logical_not(slim), zo == z)
    if way == 0:
        return in_line & (zo <= z) & (z < Z - 1)
    if way == 1:
        return in_line & (zo >= z) & (z > 0)
    if way == 2:
        return in_row & ((dx == 0) | ((dx == X - 1) & (odd == 0)))
    return in_row & ((dx == 0) | ((dx == 1) & (odd == 1)))


def kernel(
    g_hbm, ids_hbm, logits_hbm, h_hbm, w_hbm, r_hbm,
    st_out, rn_out, pk_out,
    bulk, slim, prod, cross, hbuf, wbuf, acc, sent_scores,
    ids_v, logits_v, picked_v, st, rn, pk,
    load_sem, send_sem, recv_sem, cross_send, cross_recv,
    score_send, score_recv, r_send, r_recv, pk_send, pk_recv,
):
    sections = lax.axis_size("pp")
    s = lax.axis_index("pp")
    me = lax.axis_index("ep")
    core = lax.rem(me, CORES)
    chip = lax.div(me, CORES)
    x, z = lax.div(chip, Z), lax.rem(chip, Z)

    def at(xx, zz, cc=core):
        return (xx * Z + zz) * CORES + cc

    right, left = lax.rem(x + 1, X), lax.rem(x + X - 1, X)
    across = lax.rem(x + 2, X)
    sibling = (s, at(x, z, 1 - core))
    target = (
        (s, at(x, jnp.minimum(z + 1, Z - 1))),
        (s, at(x, jnp.maximum(z - 1, 0))),
        (s, at(right, z)),
        (s, at(left, z)),
    )
    opposite = (s, at(across, z))
    below = jnp.maximum(s - 1, 0)
    above = jnp.minimum(s + 1, sections - 1)

    def load(k, src, dst):
        return pltpu.make_async_copy(src, dst, load_sem.at[k])

    loads = [
        load(0, g_hbm.at[:, pl.ds(0, BULK)], bulk.at[chip]),
        load(1, g_hbm.at[:, pl.ds(BULK, SLIM)], slim.at[chip, pl.ds(0, TOK)]),
        load(2, ids_hbm, ids_v),
        load(3, logits_hbm, logits_v),
        load(4, h_hbm.at[:, 1 - core], hbuf.at[0]),
        load(5, w_hbm.at[:, pl.ds(0, HALF)], wbuf.at[:, pl.ds(0, HALF)]),
        load(6, w_hbm.at[:, pl.ds(HALF, HALF)], wbuf.at[:, pl.ds(HALF, HALF)]),
        load(7, h_hbm.at[:, core], hbuf.at[1]),
    ]
    for copy in loads:
        copy.start()

    barrier = pltpu.get_barrier_semaphore()

    def greet(device):
        pl.semaphore_signal(barrier, inc=1, device_id=device, device_id_type=MESH)

    for device in (target[2], target[3], opposite, sibling):
        greet(device)

    @pl.when(z < Z - 1)
    def _():
        greet(target[0])

    @pl.when(z > 0)
    def _():
        greet(target[1])

    @pl.when(s > 0)
    def _():
        @pl.loop(0, CHIPS)
        def _(q):
            greet((below, q * CORES + core))

    @pl.when(s < sections - 1)
    def _():
        @pl.loop(0, CHIPS)
        def _(q):
            greet((above, q * CORES + core))

    calls = 4 + (z < Z - 1).astype(jnp.int32) + (z > 0).astype(jnp.int32)
    calls = calls + CHIPS * ((s > 0).astype(jnp.int32) + (s < sections - 1).astype(jnp.int32))
    pl.semaphore_wait(barrier, calls)

    def remote(src, dst, send, recv, device):
        return pltpu.make_async_remote_copy(
            src_ref=src, dst_ref=dst, send_sem=send, recv_sem=recv,
            device_id=device, device_id_type=MESH,
        )

    def wide_piece(q, piece):
        return bulk.at[q, :, pl.ds(pl.multiple_of(piece * WIDE, 128), WIDE)]

    def piece_ref(q, kind, piece):
        if kind == 0:
            return wide_piece(q, piece)
        if kind == 1:
            return slim.at[q]
        return bulk.at[q, :, pl.ds(2 * WIDE, SLIM)]

    def passing(way, q, kind, piece):
        ref = piece_ref(q, kind, piece)
        return remote(ref, ref, send_sem.at[way, q, piece], recv_sem.at[q, piece], target[way])

    def pass_on(q, kind, piece):
        xo, zo = lax.div(q, Z), lax.rem(q, Z)
        for way in range(4):

            @pl.when(goes(way, x, z, xo, zo, piece))
            def _(way=way):
                passing(way, q, kind, piece).start()

    rows = pl.ds(pl.multiple_of(core * RANK_ROWS, RANK_ROWS), RANK_ROWS)

    def quarter(xx):
        return pl.ds(pl.multiple_of(xx * QUARTER, 128), QUARTER)

    router_down = remote(
        r_hbm.at[rows, quarter(x)], rn.at[rows, quarter(x)], r_send.at[0], r_recv.at[0], (below, me)
    )

    @pl.when(s > 0)
    def _():
        router_down.start()

    loads[0].wait()
    pass_on(chip, 0, 0)
    pass_on(chip, 0, 1)

    for k in (1, 2, 3):
        loads[k].wait()
    lanes = lax.broadcasted_iota(jnp.int32, (TOK, 128), 1)
    ids = ids_v[...]
    marks = jnp.zeros((TOK, 128), F32)
    for k in range(ids.shape[1]):
        marks = marks + (ids[:, k : k + 1] == lanes).astype(F32)
    named = marks.T[:EXPERTS]
    upper = (
        lax.broadcasted_iota(jnp.int32, (TOK, TOK), 0)
        < lax.broadcasted_iota(jnp.int32, (TOK, TOK), 1)
    ).astype(BF16)
    before = jnp.dot(named.astype(BF16), upper, preferred_element_type=F32)
    ranks = jnp.where(named > 0, before, -1.0).astype(BF16)
    slim[chip, TOK : TOK + RANK_ROWS, :] = jnp.concatenate(
        [ranks[:RANK_ROWS], ranks[RANK_ROWS:], jnp.zeros((RANK_ROWS, SLIM - 2 * TOK), BF16)], axis=1
    )
    pass_on(chip, 1, 2)
    pass_on(chip, 2, 3)
    logits = jnp.concatenate([logits_v[...], jnp.zeros((TOK, 128 - EXPERTS), F32)], axis=1)
    affinity = 1.0 / (1.0 + jnp.exp(-logits.T[:EXPERTS]))
    picked_v[...] = jnp.where(named > 0, affinity, 0.0)
    picked_down = remote(picked_v, pk, pk_send, pk_recv, (below, me))

    @pl.when(s > 0)
    def _():
        picked_down.start()

    steps = [by_row(z, words) for words in zip(*map(packed, STEPS))]
    early = [by_row(z, words) for words in zip(*(packed(row[:EARLY]) for row in ORDER))]

    def outputs(which, half, store):
        lhs = hbuf[which].reshape(CHIPS * MOST, FFW)

        @pl.loop(0, HALF // 256)
        def _(t):
            cols = pl.ds(pl.multiple_of(half * HALF + t * 256, 256), 256)
            out = jnp.dot(lhs, wbuf[:, cols], preferred_element_type=F32)
            store(cols, out.astype(BF16).reshape(CHIPS, MOST, 256))

    def store_cross(cols, value):
        cross[:, :, cols] = value

    def store_own(cols, value):
        prod[:, core, :, cols] = value

    def crossing(half):
        cols = pl.ds(half * HALF, HALF)
        return remote(
            cross.at[:, :, cols], prod.at[:, core, :, cols],
            cross_send.at[half], cross_recv.at[half], sibling,
        )

    loads[4].wait()
    for half in range(2):
        loads[5 + half].wait()
        outputs(0, half, store_cross)
        crossing(half).start()
    loads[7].wait()
    for half in range(2):
        outputs(1, half, store_own)

    def take(q, kind, piece):
        passing(2, q, kind, piece).wait_recv()
        pass_on(q, kind, piece)

    def decode(code):
        shard = lax.rem(code, 64)
        xo = lax.rem(x + lax.div(shard, 16), X)
        zo = lax.rem(lax.div(shard, 4), Z)
        return xo * Z + zo, lax.rem(shard, 4)

    def by_kind(piece, act):
        for kind, cond in ((0, piece < 2), (1, piece == 2), (2, piece == 3)):

            @pl.when(cond)
            def _(kind=kind):
                act(kind, piece if kind == 0 else jnp.int32(kind + 1))

    @pl.loop(0, EARLY)
    def _(i):
        q, piece = decode(entry(early, i))
        by_kind(piece, functools.partial(take, q))

    def spread(k, device):
        ref = rn.at[rows, quarter(x)]
        return remote(ref, ref, r_send.at[1 + k], r_recv.at[1 + k], device)

    def came(k, xx):
        ref = rn.at[rows, quarter(xx)]
        return remote(ref, ref, r_send.at[1 + k], r_recv.at[1 + k], target[2])

    spreads = [spread(0, target[2]), spread(1, target[3]), spread(2, opposite)]
    own_rows = remote(rn.at[rows], rn.at[rows], r_send.at[4], r_recv.at[4], sibling)
    other = pl.ds(pl.multiple_of((1 - core) * RANK_ROWS, RANK_ROWS), RANK_ROWS)
    other_rows = remote(rn.at[other], rn.at[other], r_send.at[4], r_recv.at[4], sibling)

    @pl.when(s < sections - 1)
    def _():
        router_down.wait_recv()
        for copy in spreads:
            copy.start()

    for half in range(2):
        crossing(half).wait_recv()
    acc[...] = jnp.zeros_like(acc)

    def score_copy(q):
        return remote(
            sent_scores.at[q], st.at[chip], score_send.at[q], score_recv.at[chip],
            (below, q * CORES + core),
        )

    first = lax.rem(chip * CORES, RANK_ROWS)
    group = lax.div(chip * CORES, RANK_ROWS)

    def score(q, kind, piece):
        if kind == 0:
            cols = pl.ds(pl.multiple_of(piece * WIDE, 128), WIDE)
            block = bulk[q, :, cols]
        elif kind == 1:
            cols = pl.ds(BULK, SLIM)
            block = slim[q, :TOK, :]
        else:
            cols = pl.ds(2 * WIDE, SLIM)
            block = bulk[q, :, cols]
        lhs = prod[q, :, :, cols].reshape(CORES * MOST, block.shape[1])
        acc[q] += lax.dot_general(
            lhs, block, (((1,), (1,)), ((), ())), preferred_element_type=F32
        )

    def finish(q):
        lane0 = pl.ds(pl.multiple_of(group * TOK, TOK), TOK)
        held = slim[q, pl.ds(TOK, RANK_ROWS), lane0].astype(F32)
        line = lax.broadcasted_iota(jnp.int32, (RANK_ROWS, TOK), 0)
        slot = lax.broadcasted_iota(jnp.int32, (MOST, TOK), 0).astype(F32)
        total = acc[q]
        tile = lax.broadcasted_iota(jnp.int32, (8, TOK), 0)
        result = jnp.zeros((8, TOK), F32)
        for e in range(CORES):
            rank = jnp.sum(jnp.where(line == first + e, held, 0.0), axis=0, keepdims=True)
            part = total[e * MOST : (e + 1) * MOST]
            row = jnp.sum(jnp.where(slot == rank, part, 0.0), axis=0, keepdims=True)
            result = jnp.where(tile == e, row, result)
        sent_scores[q] = result

        @pl.when(s > 0)
        def _():
            score_copy(q).start()

    @pl.loop(0, COUNT)
    def _(i):
        code = entry(steps, i)
        q, piece = decode(code)
        new = lax.rem(lax.div(code, 64), 2) == 1

        def step(kind, which):
            @pl.when(new)
            def _():
                take(q, kind, which)

            score(q, kind, which)

        by_kind(piece, step)

        @pl.when(code >= 128)
        def _():
            finish(q)

        @pl.when((i == COUNT // 2) & (s < sections - 1))
        def _():
            came(0, left).wait_recv()
            came(1, right).wait_recv()
            came(2, across).wait_recv()
            own_rows.start()

    @pl.when(s < sections - 1)
    def _():
        other_rows.wait_recv()
        rn_out[...] = rn[...]
        picked_down.wait_recv()
        pk_out[...] = pk[...]

        @pl.loop(0, CHIPS)
        def _(q):
            remote(
                sent_scores.at[q], st.at[q], score_send.at[q], score_recv.at[q], (below, me)
            ).wait_recv()

        st_out[...] = st[...]

    @pl.when(s == sections - 1)
    def _():
        rn_out[...] = jnp.zeros_like(rn_out)
        pk_out[...] = jnp.zeros_like(pk_out)
        st_out[...] = jnp.zeros_like(st_out)

    for half in range(2):
        crossing(half).wait_send()

    @pl.when(s < sections - 1)
    def _():
        for copy in spreads:
            copy.wait_send()
        own_rows.wait_send()

    @pl.when(s > 0)
    def _():
        router_down.wait_send()
        picked_down.wait_send()

        @pl.loop(0, CHIPS)
        def _(q):
            score_copy(q).wait_send()

    @pl.loop(0, CHIPS)
    def _(q):
        xo, zo = lax.div(q, Z), lax.rem(q, Z)
        for kind, pieces in ((0, (0, 1)), (1, (2,)), (2, (3,))):
            for piece in pieces:
                for way in range(4):

                    @pl.when(goes(way, x, z, xo, zo, piece))
                    def _(kind=kind, piece=piece, way=way):
                        passing(way, q, kind, piece).wait_send()


def exchange(g, ids, logits, h, w, r):
    vmem = pl.BlockSpec(memory_space=pltpu.VMEM)
    dma = pltpu.SemaphoreType.DMA
    return pl.pallas_call(
        kernel,
        out_shape=(
            jax.ShapeDtypeStruct((CHIPS, 8, TOK), F32),
            jax.ShapeDtypeStruct((EXPERTS, D), BF16),
            jax.ShapeDtypeStruct((EXPERTS, TOK), F32),
        ),
        in_specs=[pl.BlockSpec(memory_space=pl.ANY)] * 6,
        out_specs=(vmem,) * 3,
        scratch_shapes=[
            pltpu.VMEM((CHIPS, TOK, BULK), BF16),
            pltpu.VMEM((CHIPS, TOK + RANK_ROWS, SLIM), BF16),
            pltpu.VMEM((CHIPS, CORES, MOST, D), BF16),
            pltpu.VMEM((CHIPS, MOST, D), BF16),
            pltpu.VMEM((CORES, CHIPS, MOST, FFW), BF16),
            pltpu.VMEM((FFW, D), BF16),
            pltpu.VMEM((CHIPS, CORES * MOST, TOK), F32),
            pltpu.VMEM((CHIPS, 8, TOK), F32),
            pltpu.VMEM(ids.shape, jnp.int32),
            pltpu.VMEM(logits.shape, F32),
            pltpu.VMEM((EXPERTS, TOK), F32),
            pltpu.VMEM((CHIPS, 8, TOK), F32),
            pltpu.VMEM((EXPERTS, D), BF16),
            pltpu.VMEM((EXPERTS, TOK), F32),
            dma((8,)),
            dma((4, CHIPS, 4)),
            dma((CHIPS, 4)),
            dma((2,)),
            dma((2,)),
            dma((CHIPS,)),
            dma((CHIPS,)),
            dma((5,)),
            dma((5,)),
            dma,
            dma,
        ],
        compiler_params=pltpu.CompilerParams(
            collective_id=0, has_side_effects=True, vmem_limit_bytes=58 * 2**20
        ),
    )(g, ids, logits, h, w, r)


def on_device(out_grads, expert_ids, router_logits, hidden_acts, w_down, w_router):
    h = hidden_acts.reshape(CHIPS, CORES, MOST, FFW)
    scores, router, picked = exchange(
        out_grads[0], expert_ids[0], router_logits[0], h, w_down[0, 0], w_router[0]
    )
    score_grad = scores[:, :CORES].reshape(EXPERTS, TOK)
    picked_sum = jnp.sum(picked, axis=0, keepdims=True)
    mean_grad = jnp.sum(picked / picked_sum * score_grad, axis=0, keepdims=True)
    table = (score_grad - mean_grad) / picked_sum * picked * (1.0 - picked)
    last = lax.axis_index("pp") == lax.axis_size("pp") - 1
    table = jnp.where(last, 0.0, table).astype(BF16)
    result = lax.dot_general(table, router, (((0,), (0,)), ((), ())), preferred_element_type=F32)
    return result.astype(BF16)[None]


def solution(mesh):
    in_specs = (
        P("pp", "ep", None),
        P("pp", "ep", None),
        P("pp", "ep", None),
        P("pp", "ep", None, None),
        P("pp", "ep", None, None),
        P("pp", None, None),
    )
    out_specs = P("pp", "ep", None)
    return jax.shard_map(
        on_device, mesh=mesh, in_specs=in_specs, out_specs=out_specs, check_vma=False
    )
```

```python
import functools

import jax
import jax.numpy as jnp
from jax import lax
from jax.experimental import pallas as pl
from jax.experimental.pallas import tpu as pltpu
from jax.sharding import PartitionSpec as P

MESH = pl.DeviceIdType.MESH
F32, BF16 = jnp.float32, jnp.bfloat16

X, Z, CORES = 4, 4, 2
CHIPS = X * Z
TOK, D, FFW, MOST, EXPERTS = 128, 3584, 1024, 48, 32
BOTH = CORES * MOST
WIDE, SLIM = 1408, 384
RANKS = 4
RANK_ROWS, RANK_LANES = 16, 256
QUARTER = D // X
HALF = D // 2

ORDER = (
    (
        12, 36, 100, 32, 8, 96, 97, 33, 9, 98, 34, 10, 99, 68, 108, 35, 44, 11, 20, 64, 40, 16, 65, 104, 17,
        106, 105, 42, 41, 18, 66, 76, 116, 67, 52, 107, 43, 19, 28, 48, 112, 24, 72, 49, 113, 25, 84, 73, 124, 60,
        114, 50, 26, 80, 56, 115, 51, 27, 74, 81, 75, 120, 122, 58, 123, 59, 121, 57, 92, 82, 83, 90, 91, 88, 89,
    ),
    (
        4, 20, 44, 108, 40, 0, 16, 104, 105, 41, 1, 17, 106, 42, 2, 18, 107, 76, 100, 116, 43, 36, 52, 3, 19,
        28, 98, 34, 72, 32, 99, 24, 35, 48, 96, 25, 73, 114, 112, 50, 26, 66, 115, 33, 67, 97, 51, 27, 113, 49,
        74, 68, 84, 75, 124, 122, 60, 58, 123, 59, 56, 120, 82, 83, 64, 57, 121, 65, 80, 81, 92, 90, 91, 89, 88,
    ),
    (
        12, 28, 52, 116, 48, 8, 24, 112, 113, 49, 9, 25, 114, 50, 10, 26, 115, 84, 108, 124, 51, 44, 60, 11, 27,
        4, 122, 58, 80, 40, 123, 0, 59, 56, 104, 1, 81, 106, 120, 42, 2, 90, 107, 41, 91, 105, 43, 3, 121, 57,
        82, 76, 92, 83, 100, 98, 36, 34, 99, 35, 32, 96, 74, 75, 72, 33, 97, 73, 88, 89, 68, 66, 67, 65, 64,
    ),
    (
        20, 60, 124, 56, 16, 120, 121, 57, 17, 122, 58, 18, 123, 92, 116, 59, 52, 19, 12, 88, 48, 8, 89, 112, 9,
        114, 113, 50, 49, 10, 90, 84, 108, 91, 44, 115, 51, 11, 4, 40, 104, 0, 80, 41, 105, 1, 76, 81, 100, 36,
        106, 42, 2, 72, 32, 107, 43, 3, 82, 73, 83, 96, 98, 34, 99, 35, 97, 33, 68, 74, 75, 66, 67, 64, 65,
    ),
)
EARLY = 14


def programme(z):
    late = [8 * z + p for p in range(4)] + [code for code in ORDER[z][:EARLY] if code % 8 != RANKS]
    steps = []
    for code in ORDER[z][EARLY:]:
        if late:
            steps.append(late.pop(0))
        steps.append(code + 128)
    left = {}
    for code in steps:
        left[code % 128 // 8] = left.get(code % 128 // 8, 0) + 1
    out = []
    for code in steps:
        shard = code % 128 // 8
        left[shard] -= 1
        out.append(code + (256 if left[shard] == 0 else 0))
    return out


STEPS = [programme(z) for z in range(Z)]
COUNT = max(map(len, STEPS))
IDLE = 5
STEPS = [steps + [IDLE] * (COUNT - len(steps)) for steps in STEPS]


def packed(codes):
    words = []
    for k in range(0, len(codes), 3):
        words.append(sum(code << (9 * j) for j, code in enumerate(codes[k : k + 3])))
    return words


def by_row(z, values):
    picked = jnp.int32(values[Z - 1])
    for row in range(Z - 1):
        picked = jnp.where(z == row, jnp.int32(values[row]), picked)
    return picked


def entry(words, i):
    place = lax.div(i, 3)
    while len(words) > 1:
        odd = lax.rem(place, 2) == 1
        halved = []
        for k in range(0, len(words), 2):
            more = k + 1 < len(words)
            halved.append(jnp.where(odd, words[k + 1], words[k]) if more else words[k])
        words, place = halved, lax.div(place, 2)
    turn = lax.rem(i, 3)
    scale = jnp.where(turn == 0, 1, jnp.where(turn == 1, 1 << 9, 1 << 18))
    return lax.rem(lax.div(words[0], scale), 512)


UP, DOWN, RIGHT, LEFT = range(4)


def goes(kind, x, z, xo, zo, piece):
    dx = lax.rem(xo - x + X, X)
    even = lax.rem(piece, 2) == 0
    odd = jnp.logical_not(even)
    up, down = (zo <= z) & (z < Z - 1), (zo >= z) & (z > 0)
    from_left, from_right = dx == X - 1, dx == 1
    here = dx == 0
    no = z < 0
    if kind == 2:
        return (here & up, here & down, here | from_left, here), (no,) * 4
    if kind == 0:
        whole = (here & up, here & down, here & even, here & odd)
        return whole, (no, no, (here & odd) | (from_left & even), (here & even) | (from_right & odd))
    row = zo == z
    across = row & (here | (from_left & even)), row & (here | (from_right & odd))
    return (up & (z != Z - 2), down & (z != 1), *across), (up & (z == Z - 2), down & (z == 1), no, no)


def arrives_whole(kind, x, z, xo, zo, piece):
    dx = lax.rem(xo - x + X, X)
    even = lax.rem(piece, 2) == 0
    if kind == 0:
        return (dx == 0) | ((dx == X - 1) & even) | ((dx == 1) & jnp.logical_not(even))
    return (zo == z) | ((z > 0) & (z < Z - 1))


def kernel(
    g_hbm, ids_hbm, logits_hbm, h_hbm, w_hbm, r_hbm,
    table_out, rn_out,
    held, ranks_of, wide_rows, slim_rows, prod, cross, hbuf, wbuf, acc, slot_acc, sent_scores,
    ids_v, logits_v, picked_v, st, rn, pk,
    load_sem, send_sem, recv_sem, cross_send, cross_recv,
    score_send, score_recv, r_send, r_recv, pk_send, pk_recv,
):
    sections = lax.axis_size("pp")
    s = lax.axis_index("pp")
    me = lax.axis_index("ep")
    core = lax.rem(me, CORES)
    chip = lax.div(me, CORES)
    x, z = lax.div(chip, Z), lax.rem(chip, Z)

    def at(xx, zz, cc=core):
        return (xx * Z + zz) * CORES + cc

    right, left = lax.rem(x + 1, X), lax.rem(x + X - 1, X)
    across = lax.rem(x + 2, X)
    sibling = (s, at(x, z, 1 - core))
    target = (
        (s, at(x, jnp.minimum(z + 1, Z - 1))),
        (s, at(x, jnp.maximum(z - 1, 0))),
        (s, at(right, z)),
        (s, at(left, z)),
    )
    opposite = (s, at(across, z))
    below = jnp.maximum(s - 1, 0)
    above = jnp.minimum(s + 1, sections - 1)

    def load(k, src, dst):
        return pltpu.make_async_copy(src, dst, load_sem.at[k])

    loads = [
        load(0, g_hbm, held.at[chip]),
        load(1, ids_hbm, ids_v),
        load(2, logits_hbm, logits_v),
        load(3, h_hbm.at[:, 1 - core], hbuf.at[0]),
        load(4, w_hbm.at[:, pl.ds(0, HALF)], wbuf.at[:, pl.ds(0, HALF)]),
        load(5, w_hbm.at[:, pl.ds(HALF, HALF)], wbuf.at[:, pl.ds(HALF, HALF)]),
        load(6, h_hbm.at[:, core], hbuf.at[1]),
    ]
    for copy in loads:
        copy.start()

    barrier = pltpu.get_barrier_semaphore()

    def greet(device):
        pl.semaphore_signal(barrier, inc=1, device_id=device, device_id_type=MESH)

    for device in (target[2], target[3], opposite, sibling):
        greet(device)

    @pl.when(z < Z - 1)
    def _():
        greet(target[0])

    @pl.when(z > 0)
    def _():
        greet(target[1])

    @pl.when(s < sections - 1)
    def _():
        @pl.loop(0, CHIPS)
        def _(q):
            greet((above, q * CORES + core))

    loads[1].wait()
    loads[2].wait()
    experts = lax.broadcasted_iota(jnp.int32, (EXPERTS, TOK), 0)
    ids = ids_v[...]
    named = jnp.zeros((EXPERTS, TOK), F32)
    for k in range(ids.shape[0]):
        named = named + (ids[k : k + 1] == experts).astype(F32)
    upper = (
        lax.broadcasted_iota(jnp.int32, (TOK, TOK), 0)
        < lax.broadcasted_iota(jnp.int32, (TOK, TOK), 1)
    ).astype(BF16)
    before = jnp.dot(named.astype(BF16), upper, preferred_element_type=F32)
    ranks = jnp.where(named > 0, before, -1.0).astype(BF16)
    ranks_of[chip] = jnp.concatenate([ranks[:RANK_ROWS], ranks[RANK_ROWS:]], axis=1)
    affinity = 1.0 / (1.0 + jnp.exp(-logits_v[...]))
    picked_v[...] = jnp.where(named > 0, affinity, 0.0)

    calls = 4 + (z < Z - 1).astype(jnp.int32) + (z > 0).astype(jnp.int32)
    calls = calls + CHIPS * (s > 0).astype(jnp.int32)
    pl.semaphore_wait(barrier, calls)

    def remote(src, dst, send, recv, device):
        return pltpu.make_async_remote_copy(
            src_ref=src, dst_ref=dst, send_sem=send, recv_sem=recv,
            device_id=device, device_id_type=MESH,
        )

    def lanes_of(kind, piece):
        if kind == 0:
            return pl.ds(pl.multiple_of(piece * WIDE, 128), WIDE)
        return pl.ds(pl.multiple_of(2 * WIDE + (piece - 2) * SLIM, 128), SLIM)

    def whole_ref(q, kind, piece):
        if kind == 2:
            return ranks_of.at[q]
        return held.at[q, :, lanes_of(kind, piece)]

    def rows_ref(q, kind, piece):
        if kind == 0:
            own = lax.div(q, Z) == x
            return wide_rows.at[piece, 2 * lax.rem(q, Z) + jnp.where(own, 0, 1)]
        return slim_rows.at[piece - 2, q]

    def passing(way, q, kind, piece):
        ref = whole_ref(q, kind, piece)
        return remote(ref, ref, send_sem.at[way, q, piece], recv_sem.at[q, piece], target[way])

    def passing_rows(way, q, kind, piece):
        return remote(
            rows_ref(q, kind, piece),
            held.at[q, pl.ds(0, BOTH), lanes_of(kind, piece)],
            send_sem.at[way, q, piece], recv_sem.at[q, piece], target[way],
        )

    def chosen_rows(q, of):
        group = pl.ds(pl.multiple_of(lax.div(of * CORES, RANK_ROWS) * TOK, TOK), TOK)
        table = ranks_of[q, :, group].astype(F32)
        line = lax.broadcasted_iota(jnp.int32, (RANK_ROWS, TOK), 0)
        slot = lax.broadcasted_iota(jnp.int32, (MOST, TOK), 0).astype(F32)
        first = lax.rem(of * CORES, RANK_ROWS)
        hits = []
        for e in range(CORES):
            rank = jnp.sum(jnp.where(line == first + e, table, 0.0), axis=0, keepdims=True)
            hits.append(slot == rank)
        return hits

    neighbours = (chip + 1, chip - 1, right * Z + z, left * Z + z)

    def pass_on(q, kind, piece):
        whole, some = goes(kind, x, z, lax.div(q, Z), lax.rem(q, Z), piece)
        for way in range(4):

            @pl.when(whole[way])
            def _(way=way):
                passing(way, q, kind, piece).start()

        if kind == 2:
            return
        of, any_rows = chip, z < 0
        for way in range(4):
            of = jnp.where(some[way], neighbours[way], of)
            any_rows = any_rows | some[way]

        @pl.when(any_rows)
        def _():
            pick = jnp.concatenate([hit.astype(F32) for hit in chosen_rows(q, of)], axis=0)
            rows = jnp.dot(
                pick.astype(BF16), held[q, :, lanes_of(kind, piece)], preferred_element_type=F32
            )
            rows_ref(q, kind, piece)[...] = rows.astype(BF16)
            for way in range(4):

                @pl.when(some[way])
                def _(way=way):
                    passing_rows(way, q, kind, piece).start()

    rows = pl.ds(pl.multiple_of(core * RANK_ROWS, RANK_ROWS), RANK_ROWS)

    def quarter(xx):
        return pl.ds(pl.multiple_of(xx * QUARTER, 128), QUARTER)

    router_down = remote(
        r_hbm.at[rows, quarter(x)], rn.at[rows, quarter(x)], r_send.at[0], r_recv.at[0], (below, me)
    )

    @pl.when(s > 0)
    def _():
        router_down.start()

    pass_on(chip, 2, jnp.int32(RANKS))
    loads[0].wait()
    for piece in range(4):
        pass_on(chip, piece // 2, jnp.int32(piece))
    picked_down = remote(picked_v, pk, pk_send, pk_recv, (below, me))

    @pl.when(s > 0)
    def _():
        picked_down.start()

    steps = [by_row(z, words) for words in zip(*map(packed, STEPS))]
    early = [by_row(z, words) for words in zip(*(packed(row[:EARLY]) for row in ORDER))]

    def outputs(which, half, store):
        lhs = hbuf[which].reshape(CHIPS * MOST, FFW)

        @pl.loop(0, HALF // 256)
        def _(t):
            cols = pl.ds(pl.multiple_of(half * HALF + t * 256, 256), 256)
            out = jnp.dot(lhs, wbuf[:, cols], preferred_element_type=F32)
            store(cols, out.astype(BF16).reshape(CHIPS, MOST, 256))

    def store_cross(cols, value):
        cross[:, :, cols] = value

    def store_own(cols, value):
        prod[:, core, :, cols] = value

    def crossing(half):
        cols = pl.ds(half * HALF, HALF)
        return remote(
            cross.at[:, :, cols], prod.at[:, core, :, cols],
            cross_send.at[half], cross_recv.at[half], sibling,
        )

    loads[3].wait()
    for half in range(2):
        loads[4 + half].wait()
        outputs(0, half, store_cross)
        crossing(half).start()
    loads[6].wait()
    for half in range(2):
        outputs(1, half, store_own)

    def take(q, kind, piece):
        if kind == 2:
            passing(RIGHT, q, kind, piece).wait_recv()
        else:
            full = arrives_whole(kind, x, z, lax.div(q, Z), lax.rem(q, Z), piece)

            @pl.when(full)
            def _():
                passing(RIGHT, q, kind, piece).wait_recv()

            @pl.when(jnp.logical_not(full))
            def _():
                passing_rows(RIGHT, q, kind, piece).wait_recv()

        pass_on(q, kind, piece)

    def decode(code):
        shard = lax.rem(code, 128)
        xo = lax.rem(x + lax.div(shard, 32), X)
        zo = lax.rem(lax.div(shard, 8), Z)
        return xo * Z + zo, lax.rem(shard, 8)

    def by_kind(piece, act):
        for kind, cond in ((0, piece < 2), (1, (piece == 2) | (piece == 3)), (2, piece == RANKS)):

            @pl.when(cond)
            def _(kind=kind):
                act(kind, piece)

    @pl.loop(0, EARLY)
    def _(i):
        q, piece = decode(entry(early, i))
        by_kind(piece, functools.partial(take, q))

    def spread(k, device):
        ref = rn.at[rows, quarter(x)]
        return remote(ref, ref, r_send.at[1 + k], r_recv.at[1 + k], device)

    def came(k, xx):
        ref = rn.at[rows, quarter(xx)]
        return remote(ref, ref, r_send.at[1 + k], r_recv.at[1 + k], target[2])

    spreads = [spread(0, target[2]), spread(1, target[3]), spread(2, opposite)]
    own_rows = remote(rn.at[rows], rn.at[rows], r_send.at[4], r_recv.at[4], sibling)
    other = pl.ds(pl.multiple_of((1 - core) * RANK_ROWS, RANK_ROWS), RANK_ROWS)
    other_rows = remote(rn.at[other], rn.at[other], r_send.at[4], r_recv.at[4], sibling)

    @pl.when(s < sections - 1)
    def _():
        router_down.wait_recv()
        for copy in spreads:
            copy.start()

    for half in range(2):
        crossing(half).wait_recv()
    acc[...] = jnp.zeros_like(acc)
    slot_acc[...] = jnp.zeros_like(slot_acc)

    def score_copy(q):
        return remote(
            sent_scores.at[q], st.at[chip], score_send.at[q], score_recv.at[chip],
            (below, q * CORES + core),
        )

    def score(q, kind, piece):
        cols = lanes_of(kind, piece)
        width = (WIDE, SLIM)[kind]
        full = arrives_whole(kind, x, z, lax.div(q, Z), lax.rem(q, Z), piece)

        @pl.when(full)
        def _():
            acc[q] += lax.dot_general(
                prod[q, :, :, cols].reshape(BOTH, width), held[q, :, cols],
                (((1,), (1,)), ((), ())), preferred_element_type=F32,
            )

        @pl.when(jnp.logical_not(full))
        def _():
            terms = prod[q, :, :, cols].reshape(BOTH, width).astype(F32)
            terms = terms * held[q, :BOTH, cols].astype(F32)
            total = slot_acc[q]
            for k in range(0, width, TOK):
                total = total + terms[:, k : k + TOK]
            slot_acc[q] = total

    def finish(q):
        total = acc[q] + jnp.sum(slot_acc[q], axis=1, keepdims=True)
        tile = lax.broadcasted_iota(jnp.int32, (8, TOK), 0)
        result = jnp.zeros((8, TOK), F32)
        for e, hit in enumerate(chosen_rows(q, chip)):
            part = total[e * MOST : (e + 1) * MOST]
            row = jnp.sum(jnp.where(hit, part, 0.0), axis=0, keepdims=True)
            result = jnp.where(tile == e, row, result)
        sent_scores[q] = result

        @pl.when(s > 0)
        def _():
            score_copy(q).start()

    @pl.loop(0, COUNT)
    def _(i):
        code = entry(steps, i)
        q, piece = decode(code)
        new = lax.rem(lax.div(code, 128), 2) == 1

        def step(kind, which):
            @pl.when(new)
            def _():
                take(q, kind, which)

            if kind < 2:
                score(q, kind, which)

        by_kind(piece, step)

        @pl.when(code >= 256)
        def _():
            finish(q)

        @pl.when((i == COUNT // 2) & (s < sections - 1))
        def _():
            came(0, left).wait_recv()
            came(1, right).wait_recv()
            came(2, across).wait_recv()
            own_rows.start()

    @pl.when(s < sections - 1)
    def _():
        other_rows.wait_recv()
        rn_out[...] = rn[...]
        picked_down.wait_recv()

        @pl.loop(0, CHIPS)
        def _(q):
            remote(
                sent_scores.at[q], st.at[q], score_send.at[q], score_recv.at[q], (below, me)
            ).wait_recv()

        picked = pk[...]
        score_grad = jnp.concatenate([st[q, :CORES] for q in range(CHIPS)], axis=0)
        picked_sum = jnp.sum(picked, axis=0, keepdims=True)
        mean_grad = jnp.sum(picked / picked_sum * score_grad, axis=0, keepdims=True)
        table = (score_grad - mean_grad) / picked_sum * picked * (1.0 - picked)
        square = jnp.concatenate([table, jnp.zeros((TOK - EXPERTS, TOK), F32)], axis=0)
        table_out[...] = square.T[:, :EXPERTS].astype(BF16)

    @pl.when(s == sections - 1)
    def _():
        rn_out[...] = jnp.zeros_like(rn_out)
        table_out[...] = jnp.zeros_like(table_out)

    for half in range(2):
        crossing(half).wait_send()

    @pl.when(s < sections - 1)
    def _():
        for copy in spreads:
            copy.wait_send()
        own_rows.wait_send()

    @pl.when(s > 0)
    def _():
        router_down.wait_send()
        picked_down.wait_send()

        @pl.loop(0, CHIPS)
        def _(q):
            score_copy(q).wait_send()

    @pl.loop(0, CHIPS)
    def _(q):
        for kind, pieces in ((0, (0, 1)), (1, (2, 3)), (2, (RANKS,))):
            for piece in pieces:
                whole, some = goes(kind, x, z, lax.div(q, Z), lax.rem(q, Z), jnp.int32(piece))
                for way in range(4):

                    @pl.when(whole[way])
                    def _(kind=kind, piece=piece, way=way):
                        passing(way, q, kind, jnp.int32(piece)).wait_send()

                    if kind < 2:

                        @pl.when(some[way])
                        def _(kind=kind, piece=piece, way=way):
                            passing_rows(way, q, kind, jnp.int32(piece)).wait_send()


def exchange(g, ids, logits, h, w, r):
    vmem = pl.BlockSpec(memory_space=pltpu.VMEM)
    dma = pltpu.SemaphoreType.DMA
    return pl.pallas_call(
        kernel,
        out_shape=(
            jax.ShapeDtypeStruct((TOK, EXPERTS), BF16),
            jax.ShapeDtypeStruct((EXPERTS, D), BF16),
        ),
        in_specs=[pl.BlockSpec(memory_space=pl.ANY)] * 6,
        out_specs=(vmem,) * 2,
        scratch_shapes=[
            pltpu.VMEM((CHIPS, TOK, D), BF16),
            pltpu.VMEM((CHIPS, RANK_ROWS, RANK_LANES), BF16),
            pltpu.VMEM((2, 2 * Z, BOTH, WIDE), BF16),
            pltpu.VMEM((2, CHIPS, BOTH, SLIM), BF16),
            pltpu.VMEM((CHIPS, CORES, MOST, D), BF16),
            pltpu.VMEM((CHIPS, MOST, D), BF16),
            pltpu.VMEM((CORES, CHIPS, MOST, FFW), BF16),
            pltpu.VMEM((FFW, D), BF16),
            pltpu.VMEM((CHIPS, BOTH, TOK), F32),
            pltpu.VMEM((CHIPS, BOTH, TOK), F32),
            pltpu.VMEM((CHIPS, 8, TOK), F32),
            pltpu.VMEM(ids.shape, jnp.int32),
            pltpu.VMEM(logits.shape, F32),
            pltpu.VMEM((EXPERTS, TOK), F32),
            pltpu.VMEM((CHIPS, 8, TOK), F32),
            pltpu.VMEM((EXPERTS, D), BF16),
            pltpu.VMEM((EXPERTS, TOK), F32),
            dma((7,)),
            dma((4, CHIPS, 5)),
            dma((CHIPS, 5)),
            dma((2,)),
            dma((2,)),
            dma((CHIPS,)),
            dma((CHIPS,)),
            dma((5,)),
            dma((5,)),
            dma,
            dma,
        ],
        compiler_params=pltpu.CompilerParams(
            collective_id=0, has_side_effects=True, vmem_limit_bytes=58 * 2**20
        ),
    )(g, ids, logits, h, w, r)


def on_device(out_grads, expert_ids, router_logits, hidden_acts, w_down, w_router):
    h = hidden_acts.reshape(CHIPS, CORES, MOST, FFW)
    table, router = exchange(
        out_grads[0], expert_ids[0].T, router_logits[0].T, h, w_down[0, 0], w_router[0]
    )
    return jnp.dot(table, router, preferred_element_type=F32).astype(BF16)[None]


def solution(mesh):
    in_specs = (
        P("pp", "ep", None),
        P("pp", "ep", None),
        P("pp", "ep", None),
        P("pp", "ep", None, None),
        P("pp", "ep", None, None),
        P("pp", None, None),
    )
    out_specs = P("pp", "ep", None)
    return jax.shard_map(
        on_device, mesh=mesh, in_specs=in_specs, out_specs=out_specs, check_vma=False
    )
```

```python
import functools

import jax
import jax.numpy as jnp
from jax import lax
from jax.experimental import pallas as pl
from jax.experimental.pallas import tpu as pltpu
from jax.sharding import PartitionSpec as P

MESH = pl.DeviceIdType.MESH
F32, BF16 = jnp.float32, jnp.bfloat16

X, Z, CORES = 4, 4, 2
CHIPS = X * Z
TOK, D, FFW, MOST, EXPERTS = 128, 3584, 1024, 48, 32
BOTH = CORES * MOST
WIDTH = (1408, 1408, 384, 384)
OFFSET = (0, 1408, 2816, 3200)
RANKS = 4
RANK_ROWS, RANK_LANES = 16, 256
QUARTER = D // X
HALF = D // 2

ORDER = (
    (
        12, 36, 100, 32, 8, 96, 97, 33, 9, 98, 34, 10, 99, 68, 108, 35, 44, 11, 20, 64, 40, 16, 65, 104, 17,
        106, 105, 42, 41, 18, 66, 76, 116, 67, 52, 107, 43, 19, 28, 48, 112, 24, 72, 49, 113, 25, 84, 73, 124, 60,
        114, 50, 26, 80, 56, 115, 51, 27, 74, 81, 75, 120, 122, 58, 123, 59, 121, 57, 92, 82, 83, 90, 91, 88, 89,
    ),
    (
        4, 20, 44, 108, 40, 0, 16, 104, 105, 41, 1, 17, 106, 42, 2, 18, 107, 76, 100, 116, 43, 36, 52, 3, 19,
        28, 98, 34, 72, 32, 99, 24, 35, 48, 96, 25, 73, 114, 112, 50, 26, 66, 115, 33, 67, 97, 51, 27, 113, 49,
        74, 68, 84, 75, 124, 122, 60, 58, 123, 59, 56, 120, 82, 83, 64, 57, 121, 65, 80, 81, 92, 90, 91, 89, 88,
    ),
    (
        12, 28, 52, 116, 48, 8, 24, 112, 113, 49, 9, 25, 114, 50, 10, 26, 115, 84, 108, 124, 51, 44, 60, 11, 27,
        4, 122, 58, 80, 40, 123, 0, 59, 56, 104, 1, 81, 106, 120, 42, 2, 90, 107, 41, 91, 105, 43, 3, 121, 57,
        82, 76, 92, 83, 100, 98, 36, 34, 99, 35, 32, 96, 74, 75, 72, 33, 97, 73, 88, 89, 68, 66, 67, 65, 64,
    ),
    (
        20, 60, 124, 56, 16, 120, 121, 57, 17, 122, 58, 18, 123, 92, 116, 59, 52, 19, 12, 88, 48, 8, 89, 112, 9,
        114, 113, 50, 49, 10, 90, 84, 108, 91, 44, 115, 51, 11, 4, 40, 104, 0, 80, 41, 105, 1, 76, 81, 100, 36,
        106, 42, 2, 72, 32, 107, 43, 3, 82, 73, 83, 96, 98, 34, 99, 35, 97, 33, 68, 74, 75, 66, 67, 64, 65,
    ),
)
EARLY = 14


def programme(z):
    late = [8 * z + p for p in range(4)] + [code for code in ORDER[z][:EARLY] if code % 8 != RANKS]
    steps = []
    for code in ORDER[z][EARLY:]:
        if late:
            steps.append(late.pop(0))
        steps.append(code + 128)
    left = {}
    for code in steps:
        left[code % 128 // 8] = left.get(code % 128 // 8, 0) + 1
    out = []
    for code in steps:
        shard = code % 128 // 8
        left[shard] -= 1
        out.append(code + (256 if left[shard] == 0 else 0))
    return out


STEPS = [programme(z) for z in range(Z)]
COUNT = max(map(len, STEPS))
IDLE = 5
STEPS = [steps + [IDLE] * (COUNT - len(steps)) for steps in STEPS]


def packed(codes):
    words = []
    for k in range(0, len(codes), 3):
        words.append(sum(code << (9 * j) for j, code in enumerate(codes[k : k + 3])))
    return words


def by_row(z, values):
    picked = jnp.int32(values[Z - 1])
    for row in range(Z - 1):
        picked = jnp.where(z == row, jnp.int32(values[row]), picked)
    return picked


def entry(words, i):
    place = lax.div(i, 3)
    while len(words) > 1:
        odd = lax.rem(place, 2) == 1
        halved = []
        for k in range(0, len(words), 2):
            more = k + 1 < len(words)
            halved.append(jnp.where(odd, words[k + 1], words[k]) if more else words[k])
        words, place = halved, lax.div(place, 2)
    turn = lax.rem(i, 3)
    scale = jnp.where(turn == 0, 1, jnp.where(turn == 1, 1 << 9, 1 << 18))
    return lax.rem(lax.div(words[0], scale), 512)


UP, DOWN, RIGHT, LEFT = range(4)
WHOLE, ROWS = range(2)


def rem(a, b):
    return a % b if isinstance(a, int) else lax.rem(a, b)


def goes(piece, x, z, xo, zo):
    dx = rem(xo - x + X, X)
    even = piece % 2 == 0
    up, down = (zo <= z) & (z < Z - 1), (zo >= z) & (z > 0)
    here = dx == 0
    beside = dx == (X - 1 if even else 1)
    no = z < 0
    if piece == RANKS:
        return (here & up, here & down, here | beside, here), (no,) * 4
    if piece < 2:
        if even:
            return (here & up, here & down, here, no), (no, no, beside, here)
        return (here & up, here & down, no, here), (no, no, here, beside)
    row = zo == z
    across = (row & (here | beside), row & here)
    if not even:
        across = across[::-1]
    return (up & (z != Z - 2), down & (z != 1), *across), (up & (z == Z - 2), down & (z == 1), no, no)


def arrives_whole(piece, x, z, xo, zo):
    dx = rem(xo - x + X, X)
    if piece < 2:
        return (dx == 0) | (dx == (X - 1 if piece == 0 else 1))
    return (zo == z) | ((z > 0) & (z < Z - 1))


def sends(row):
    count = {}
    for q in range(CHIPS):
        for piece in range(5):
            for form, ways in enumerate(goes(piece, 0, row, q // Z, q % Z)):
                for way in range(4):
                    if ways[way]:
                        count[way, piece, form] = count.get((way, piece, form), 0) + 1
    return count


SENDS = [sends(row) for row in range(Z)]
GROUPS = sorted(set().union(*SENDS))


def kernel(
    g_hbm, ids_hbm, logits_hbm, h_hbm, w_hbm, r_hbm,
    table_out, rn_out,
    held, ranks_of, wide_rows, slim_rows, prod, cross, hbuf, wbuf, acc, slot_acc, sent_scores,
    ids_v, logits_v, picked_v, st, rn, pk,
    load_sem, send_sem, recv_sem, cross_send, cross_recv,
    score_send, score_recv, r_send, r_recv, pk_send, pk_recv,
):
    sections = lax.axis_size("pp")
    s = lax.axis_index("pp")
    me = lax.axis_index("ep")
    core = lax.rem(me, CORES)
    chip = lax.div(me, CORES)
    x, z = lax.div(chip, Z), lax.rem(chip, Z)

    def at(xx, zz, cc=core):
        return (xx * Z + zz) * CORES + cc

    right, left = lax.rem(x + 1, X), lax.rem(x + X - 1, X)
    across = lax.rem(x + 2, X)
    sibling = (s, at(x, z, 1 - core))
    target = (
        (s, at(x, jnp.minimum(z + 1, Z - 1))),
        (s, at(x, jnp.maximum(z - 1, 0))),
        (s, at(right, z)),
        (s, at(left, z)),
    )
    opposite = (s, at(across, z))
    below = jnp.maximum(s - 1, 0)
    above = jnp.minimum(s + 1, sections - 1)

    def load(k, src, dst):
        return pltpu.make_async_copy(src, dst, load_sem.at[k])

    loads = [
        load(0, g_hbm, held.at[chip]),
        load(1, ids_hbm, ids_v),
        load(2, logits_hbm, logits_v),
        load(3, h_hbm.at[:, 1 - core], hbuf.at[0]),
        load(4, w_hbm.at[:, pl.ds(0, HALF)], wbuf.at[:, pl.ds(0, HALF)]),
        load(5, w_hbm.at[:, pl.ds(HALF, HALF)], wbuf.at[:, pl.ds(HALF, HALF)]),
        load(6, h_hbm.at[:, core], hbuf.at[1]),
    ]
    for copy in loads:
        copy.start()

    barrier = pltpu.get_barrier_semaphore()

    def greet(device):
        pl.semaphore_signal(barrier, inc=1, device_id=device, device_id_type=MESH)

    for device in (target[2], target[3], opposite, sibling):
        greet(device)

    @pl.when(z < Z - 1)
    def _():
        greet(target[0])

    @pl.when(z > 0)
    def _():
        greet(target[1])

    @pl.when(s < sections - 1)
    def _():
        @pl.loop(0, CHIPS)
        def _(q):
            greet((above, q * CORES + core))

    loads[1].wait()
    loads[2].wait()
    experts = lax.broadcasted_iota(jnp.int32, (EXPERTS, TOK), 0)
    ids = ids_v[...]
    named = jnp.zeros((EXPERTS, TOK), F32)
    for k in range(ids.shape[0]):
        named = named + (ids[k : k + 1] == experts).astype(F32)
    upper = (
        lax.broadcasted_iota(jnp.int32, (TOK, TOK), 0)
        < lax.broadcasted_iota(jnp.int32, (TOK, TOK), 1)
    ).astype(BF16)
    before = jnp.dot(named.astype(BF16), upper, preferred_element_type=F32)
    ranks = jnp.where(named > 0, before, -1.0).astype(BF16)
    ranks_of[chip] = jnp.concatenate([ranks[:RANK_ROWS], ranks[RANK_ROWS:]], axis=1)
    affinity = 1.0 / (1.0 + jnp.exp(-logits_v[...]))
    picked_v[...] = jnp.where(named > 0, affinity, 0.0)

    calls = 4 + (z < Z - 1).astype(jnp.int32) + (z > 0).astype(jnp.int32)
    calls = calls + CHIPS * (s > 0).astype(jnp.int32)
    pl.semaphore_wait(barrier, calls)

    def remote(src, dst, send, recv, device):
        return pltpu.make_async_remote_copy(
            src_ref=src, dst_ref=dst, send_sem=send, recv_sem=recv,
            device_id=device, device_id_type=MESH,
        )

    def lanes_of(piece):
        return pl.ds(OFFSET[piece], WIDTH[piece])

    def whole_ref(q, piece):
        if piece == RANKS:
            return ranks_of.at[q]
        return held.at[q, :, lanes_of(piece)]

    def rows_ref(q, piece):
        if piece < 2:
            own = lax.div(q, Z) == x
            place = 2 * lax.rem(q, Z) + jnp.where(own, 0, 1)
            return wide_rows.at[place, :, lanes_of(piece)]
        return slim_rows.at[q, :, pl.ds(OFFSET[piece] - OFFSET[2], WIDTH[piece])]

    def passing(way, q, piece):
        ref = whole_ref(q, piece)
        sent = send_sem.at[GROUPS.index((way, piece, WHOLE))]
        return remote(ref, ref, sent, recv_sem.at[q, piece], target[way])

    def passing_rows(way, q, piece):
        return remote(
            rows_ref(q, piece), held.at[q, pl.ds(0, BOTH), lanes_of(piece)],
            send_sem.at[GROUPS.index((way, piece, ROWS))], recv_sem.at[q, piece], target[way],
        )

    def chosen_rows(q, of):
        group = pl.ds(pl.multiple_of(lax.div(of * CORES, RANK_ROWS) * TOK, TOK), TOK)
        table = ranks_of[q, :, group].astype(F32)
        line = lax.broadcasted_iota(jnp.int32, (RANK_ROWS, TOK), 0)
        slot = lax.broadcasted_iota(jnp.int32, (MOST, TOK), 0).astype(F32)
        first = lax.rem(of * CORES, RANK_ROWS)
        hits = []
        for e in range(CORES):
            rank = jnp.sum(jnp.where(line == first + e, table, 0.0), axis=0, keepdims=True)
            hits.append(slot == rank)
        return hits

    neighbours = (chip + 1, chip - 1, right * Z + z, left * Z + z)

    def pass_on(q, piece):
        whole, some = goes(piece, x, z, lax.div(q, Z), lax.rem(q, Z))
        for way in range(4):
            if (way, piece, WHOLE) in GROUPS:

                @pl.when(whole[way])
                def _(way=way):
                    passing(way, q, piece).start()

        if piece == RANKS:
            return
        of, any_rows = chip, z < 0
        for way in range(4):
            of = jnp.where(some[way], neighbours[way], of)
            any_rows = any_rows | some[way]

        @pl.when(any_rows)
        def _():
            pick = jnp.concatenate([hit.astype(F32) for hit in chosen_rows(q, of)], axis=0)
            rows = jnp.dot(
                pick.astype(BF16), held[q, :, lanes_of(piece)], preferred_element_type=F32
            )
            rows_ref(q, piece)[...] = rows.astype(BF16)
            for way in range(4):
                if (way, piece, ROWS) in GROUPS:

                    @pl.when(some[way])
                    def _(way=way):
                        passing_rows(way, q, piece).start()

    rows = pl.ds(pl.multiple_of(core * RANK_ROWS, RANK_ROWS), RANK_ROWS)

    def quarter(xx):
        return pl.ds(pl.multiple_of(xx * QUARTER, 128), QUARTER)

    router_down = remote(
        r_hbm.at[rows, quarter(x)], rn.at[rows, quarter(x)], r_send.at[0], r_recv.at[0], (below, me)
    )

    @pl.when(s > 0)
    def _():
        router_down.start()

    pass_on(chip, RANKS)
    loads[0].wait()
    for piece in range(4):
        pass_on(chip, piece)
    picked_down = remote(picked_v, pk, pk_send, pk_recv, (below, me))

    @pl.when(s > 0)
    def _():
        picked_down.start()

    steps = [by_row(z, words) for words in zip(*map(packed, STEPS))]
    early = [by_row(z, words) for words in zip(*(packed(row[:EARLY]) for row in ORDER))]

    def outputs(which, half, store):
        lhs = hbuf[which].reshape(CHIPS * MOST, FFW)

        @pl.loop(0, HALF // 256)
        def _(t):
            cols = pl.ds(pl.multiple_of(half * HALF + t * 256, 256), 256)
            out = jnp.dot(lhs, wbuf[:, cols], preferred_element_type=F32)
            store(cols, out.astype(BF16).reshape(CHIPS, MOST, 256))

    def store_cross(cols, value):
        cross[:, :, cols] = value

    def store_own(cols, value):
        prod[:, core, :, cols] = value

    def crossing(half):
        cols = pl.ds(half * HALF, HALF)
        return remote(
            cross.at[:, :, cols], prod.at[:, core, :, cols],
            cross_send.at[half], cross_recv.at[half], sibling,
        )

    loads[3].wait()
    for half in range(2):
        loads[4 + half].wait()
        outputs(0, half, store_cross)
        crossing(half).start()
    loads[6].wait()
    for half in range(2):
        outputs(1, half, store_own)

    def arrived(q, piece, ref):
        remote(ref, ref, send_sem.at[0], recv_sem.at[q, piece], target[RIGHT]).wait_recv()

    def take(q, piece):
        if piece == RANKS:
            arrived(q, piece, ranks_of.at[q])
        else:
            full = arrives_whole(piece, x, z, lax.div(q, Z), lax.rem(q, Z))

            @pl.when(full)
            def _():
                arrived(q, piece, held.at[q, :, lanes_of(piece)])

            @pl.when(jnp.logical_not(full))
            def _():
                arrived(q, piece, held.at[q, pl.ds(0, BOTH), lanes_of(piece)])

        pass_on(q, piece)

    def decode(code):
        shard = lax.rem(code, 128)
        xo = lax.rem(x + lax.div(shard, 32), X)
        zo = lax.rem(lax.div(shard, 8), Z)
        return xo * Z + zo, lax.rem(shard, 8)

    def by_piece(piece, act):
        for k in range(5):

            @pl.when(piece == k)
            def _(k=k):
                act(k)

    @pl.loop(0, EARLY)
    def _(i):
        q, piece = decode(entry(early, i))
        by_piece(piece, functools.partial(take, q))

    def spread(k, device):
        ref = rn.at[rows, quarter(x)]
        return remote(ref, ref, r_send.at[1 + k], r_recv.at[1 + k], device)

    def came(k, xx):
        ref = rn.at[rows, quarter(xx)]
        return remote(ref, ref, r_send.at[1 + k], r_recv.at[1 + k], target[2])

    spreads = [spread(0, target[2]), spread(1, target[3]), spread(2, opposite)]
    own_rows = remote(rn.at[rows], rn.at[rows], r_send.at[4], r_recv.at[4], sibling)
    other = pl.ds(pl.multiple_of((1 - core) * RANK_ROWS, RANK_ROWS), RANK_ROWS)
    other_rows = remote(rn.at[other], rn.at[other], r_send.at[4], r_recv.at[4], sibling)

    @pl.when(s < sections - 1)
    def _():
        router_down.wait_recv()
        for copy in spreads:
            copy.start()

    for half in range(2):
        crossing(half).wait_recv()
    acc[...] = jnp.zeros_like(acc)
    slot_acc[...] = jnp.zeros_like(slot_acc)

    def score_copy(q):
        return remote(
            sent_scores.at[q], st.at[chip], score_send, score_recv,
            (below, q * CORES + core),
        )

    def score(q, piece):
        cols, width = lanes_of(piece), WIDTH[piece]
        full = arrives_whole(piece, x, z, lax.div(q, Z), lax.rem(q, Z))

        @pl.when(full)
        def _():
            acc[q] += lax.dot_general(
                prod[q, :, :, cols].reshape(BOTH, width), held[q, :, cols],
                (((1,), (1,)), ((), ())), preferred_element_type=F32,
            )

        @pl.when(jnp.logical_not(full))
        def _():
            terms = prod[q, :, :, cols].reshape(BOTH, width).astype(F32)
            terms = terms * held[q, :BOTH, cols].astype(F32)
            total = slot_acc[q]
            for k in range(0, width, TOK):
                total = total + terms[:, k : k + TOK]
            slot_acc[q] = total

    def finish(q):
        total = acc[q] + jnp.sum(slot_acc[q], axis=1, keepdims=True)
        lines = []
        for e, hit in enumerate(chosen_rows(q, chip)):
            part = total[e * MOST : (e + 1) * MOST]
            lines.append(jnp.sum(jnp.where(hit, part, 0.0), axis=0, keepdims=True))
        sent_scores[q] = jnp.concatenate(lines, axis=0)

        @pl.when(s > 0)
        def _():
            score_copy(q).start()

    @pl.loop(0, COUNT)
    def _(i):
        code = entry(steps, i)
        q, piece = decode(code)
        new = lax.rem(lax.div(code, 128), 2) == 1

        def step(k):
            @pl.when(new)
            def _():
                take(q, k)

            if k != RANKS:
                score(q, k)

        by_piece(piece, step)

        @pl.when(code >= 256)
        def _():
            finish(q)

        @pl.when((i == COUNT // 2) & (s < sections - 1))
        def _():
            came(0, left).wait_recv()
            came(1, right).wait_recv()
            came(2, across).wait_recv()
            own_rows.start()

    @pl.when(s < sections - 1)
    def _():
        other_rows.wait_recv()
        rn_out[...] = rn[...]
        picked_down.wait_recv()

        remote(sent_scores, st, score_send, score_recv, (below, me)).wait_recv()
        picked = pk[...]
        score_grad = jnp.concatenate([st[q] for q in range(CHIPS)], axis=0)
        picked_sum = jnp.sum(picked, axis=0, keepdims=True)
        mean_grad = jnp.sum(picked / picked_sum * score_grad, axis=0, keepdims=True)
        table = (score_grad - mean_grad) / picked_sum * picked * (1.0 - picked)
        square = jnp.concatenate([table, jnp.zeros((TOK - EXPERTS, TOK), F32)], axis=0)
        table_out[...] = square.T[:, :EXPERTS].astype(BF16)

    @pl.when(s == sections - 1)
    def _():
        rn_out[...] = jnp.zeros_like(rn_out)
        table_out[...] = jnp.zeros_like(table_out)

    for half in range(2):
        crossing(half).wait_send()

    @pl.when(s < sections - 1)
    def _():
        for copy in spreads:
            copy.wait_send()
        own_rows.wait_send()

    @pl.when(s > 0)
    def _():
        router_down.wait_send()
        picked_down.wait_send()
        remote(sent_scores, st, score_send, score_recv, (below, me)).wait_send()

    for row in range(Z):

        @pl.when(z == row)
        def _(row=row):
            for (way, piece, form), n in SENDS[row].items():
                if piece == RANKS:
                    ref = ranks_of.at[pl.ds(0, n)]
                else:
                    ref = held.at[pl.ds(0, n), pl.ds(0, (TOK, BOTH)[form]), lanes_of(piece)]
                sent = send_sem.at[GROUPS.index((way, piece, form))]
                remote(ref, ref, sent, recv_sem.at[0, 0], target[RIGHT]).wait_send()


def exchange(g, ids, logits, h, w, r):
    vmem = pl.BlockSpec(memory_space=pltpu.VMEM)
    dma = pltpu.SemaphoreType.DMA
    return pl.pallas_call(
        kernel,
        out_shape=(
            jax.ShapeDtypeStruct((TOK, EXPERTS), BF16),
            jax.ShapeDtypeStruct((EXPERTS, D), BF16),
        ),
        in_specs=[pl.BlockSpec(memory_space=pl.ANY)] * 6,
        out_specs=(vmem,) * 2,
        scratch_shapes=[
            pltpu.VMEM((CHIPS, TOK, D), BF16),
            pltpu.VMEM((CHIPS, RANK_ROWS, RANK_LANES), BF16),
            pltpu.VMEM((2 * Z, BOTH, OFFSET[2]), BF16),
            pltpu.VMEM((CHIPS, BOTH, D - OFFSET[2]), BF16),
            pltpu.VMEM((CHIPS, CORES, MOST, D), BF16),
            pltpu.VMEM((CHIPS, MOST, D), BF16),
            pltpu.VMEM((CORES, CHIPS, MOST, FFW), BF16),
            pltpu.VMEM((FFW, D), BF16),
            pltpu.VMEM((CHIPS, BOTH, TOK), F32),
            pltpu.VMEM((CHIPS, BOTH, TOK), F32),
            pltpu.VMEM((CHIPS, CORES, TOK), F32),
            pltpu.VMEM(ids.shape, jnp.int32),
            pltpu.VMEM(logits.shape, F32),
            pltpu.VMEM((EXPERTS, TOK), F32),
            pltpu.VMEM((CHIPS, CORES, TOK), F32),
            pltpu.VMEM((EXPERTS, D), BF16),
            pltpu.VMEM((EXPERTS, TOK), F32),
            dma((7,)),
            dma((len(GROUPS),)),
            dma((CHIPS, 5)),
            dma((2,)),
            dma((2,)),
            dma,
            dma,
            dma((5,)),
            dma((5,)),
            dma,
            dma,
        ],
        compiler_params=pltpu.CompilerParams(
            collective_id=0, has_side_effects=True, vmem_limit_bytes=58 * 2**20
        ),
    )(g, ids, logits, h, w, r)


def on_device(out_grads, expert_ids, router_logits, hidden_acts, w_down, w_router):
    h = hidden_acts.reshape(CHIPS, CORES, MOST, FFW)
    table, router = exchange(
        out_grads[0], expert_ids[0].T, router_logits[0].T, h, w_down[0, 0], w_router[0]
    )
    return jnp.dot(table, router, preferred_element_type=F32).astype(BF16)[None]


def solution(mesh):
    in_specs = (
        P("pp", "ep", None),
        P("pp", "ep", None),
        P("pp", "ep", None),
        P("pp", "ep", None, None),
        P("pp", "ep", None, None),
        P("pp", None, None),
    )
    out_specs = P("pp", "ep", None)
    return jax.shard_map(
        on_device, mesh=mesh, in_specs=in_specs, out_specs=out_specs, check_vma=False
    )
```

```python
import functools

import jax
import jax.numpy as jnp
from jax import lax
from jax.experimental import pallas as pl
from jax.experimental.pallas import tpu as pltpu
from jax.sharding import PartitionSpec as P

MESH = pl.DeviceIdType.MESH
F32, BF16 = jnp.float32, jnp.bfloat16

X, Z, CORES = 4, 4, 2
CHIPS = X * Z
TOK, D, FFW, MOST, EXPERTS = 128, 3584, 1024, 48, 32
BOTH = CORES * MOST
WIDTH = (1408, 1408, 384, 384)
OFFSET = (0, 1408, 2816, 3200)
RANKS = 4
RANK_ROWS, RANK_LANES = 16, 256
QUARTER = D // X
HALF = D // 2

ORDER = (
    (
        12, 36, 100, 11, 35, 99, 32, 8, 96, 33, 97, 9, 34, 98, 44, 68, 108, 10, 20, 67, 19, 43, 107, 40, 104,
        16, 64, 65, 105, 17, 41, 66, 52, 76, 116, 42, 106, 18, 28, 48, 75, 72, 27, 51, 115, 49, 112, 24, 73, 60,
        113, 84, 124, 81, 80, 25, 50, 114, 26, 56, 74, 120, 92, 59, 83, 123, 57, 58, 121, 122, 82, 91, 90, 88, 89,
    ),
    (
        4, 20, 44, 108, 3, 19, 43, 107, 40, 0, 16, 104, 41, 105, 1, 17, 42, 106, 36, 76, 52, 100, 116, 2, 18,
        28, 75, 35, 27, 99, 72, 51, 32, 34, 115, 98, 67, 48, 96, 24, 73, 112, 25, 66, 50, 97, 33, 114, 26, 113,
        49, 74, 60, 59, 68, 84, 83, 124, 123, 58, 122, 56, 64, 82, 57, 120, 65, 80, 81, 121, 92, 91, 90, 89, 88,
    ),
    (
        12, 28, 52, 116, 11, 27, 51, 115, 48, 8, 24, 112, 49, 113, 9, 25, 50, 114, 44, 84, 60, 108, 124, 10, 26,
        4, 83, 59, 3, 123, 80, 43, 40, 58, 107, 122, 91, 56, 104, 0, 81, 120, 1, 90, 42, 105, 41, 106, 2, 121,
        57, 82, 36, 35, 76, 75, 92, 100, 99, 34, 98, 32, 72, 74, 33, 96, 73, 88, 89, 97, 68, 67, 66, 65, 64,
    ),
    (
        20, 60, 124, 19, 59, 123, 56, 16, 120, 57, 121, 17, 58, 122, 52, 92, 116, 18, 12, 91, 11, 51, 115, 48, 112,
        8, 88, 89, 113, 9, 49, 90, 44, 84, 108, 50, 114, 10, 4, 40, 83, 80, 3, 43, 107, 41, 104, 0, 81, 36,
        105, 76, 100, 73, 72, 1, 42, 106, 2, 32, 82, 96, 68, 35, 75, 99, 33, 34, 97, 98, 74, 67, 66, 64, 65,
    ),
)
EARLY = 14


def programme(z):
    late = [8 * z + p for p in range(4)] + [code for code in ORDER[z][:EARLY] if code % 8 != RANKS]
    steps = []
    for code in ORDER[z][EARLY:]:
        if late:
            steps.append(late.pop(0))
        steps.append(code + 128)
    left = {}
    for code in steps:
        left[code % 128 // 8] = left.get(code % 128 // 8, 0) + 1
    out = []
    for code in steps:
        shard = code % 128 // 8
        left[shard] -= 1
        out.append(code + (256 if left[shard] == 0 else 0))
    return out


STEPS = [programme(z) for z in range(Z)]
COUNT = max(map(len, STEPS))
IDLE = 5
STEPS = [steps + [IDLE] * (COUNT - len(steps)) for steps in STEPS]


def packed(codes):
    words = []
    for k in range(0, len(codes), 3):
        words.append(sum(code << (9 * j) for j, code in enumerate(codes[k : k + 3])))
    return words


def by_row(z, values):
    picked = jnp.int32(values[Z - 1])
    for row in range(Z - 1):
        picked = jnp.where(z == row, jnp.int32(values[row]), picked)
    return picked


def entry(words, i):
    place = lax.div(i, 3)
    while len(words) > 1:
        odd = lax.rem(place, 2) == 1
        halved = []
        for k in range(0, len(words), 2):
            more = k + 1 < len(words)
            halved.append(jnp.where(odd, words[k + 1], words[k]) if more else words[k])
        words, place = halved, lax.div(place, 2)
    turn = lax.rem(i, 3)
    scale = jnp.where(turn == 0, 1, jnp.where(turn == 1, 1 << 9, 1 << 18))
    return lax.rem(lax.div(words[0], scale), 512)


UP, DOWN, RIGHT, LEFT = range(4)
WHOLE, ROWS = range(2)


def rem(a, b):
    return a % b if isinstance(a, int) else lax.rem(a, b)


def goes(piece, x, z, xo, zo):
    dx = rem(xo - x + X, X)
    even = piece % 2 == 0
    up, down = (zo <= z) & (z < Z - 1), (zo >= z) & (z > 0)
    here = dx == 0
    beside = dx == (X - 1 if even else 1)
    no = z < 0
    if piece == RANKS:
        return (here & up, here & down, here | beside, here), (no,) * 4
    if piece < 2:
        if even:
            return (here & up, here & down, here, no), (no, no, beside, here)
        return (here & up, here & down, no, here), (no, no, here, beside)
    row = zo == z
    across = (row & (here | beside), row & here)
    if not even:
        across = across[::-1]
    return (up & (z != Z - 2), down & (z != 1), *across), (up & (z == Z - 2), down & (z == 1), no, no)


def arrives_whole(piece, x, z, xo, zo):
    dx = rem(xo - x + X, X)
    if piece < 2:
        return (dx == 0) | (dx == (X - 1 if piece == 0 else 1))
    return (zo == z) | ((z > 0) & (z < Z - 1))


def sends(row):
    count = {}
    for q in range(CHIPS):
        for piece in range(5):
            for form, ways in enumerate(goes(piece, 0, row, q // Z, q % Z)):
                for way in range(4):
                    if ways[way]:
                        count[way, piece, form] = count.get((way, piece, form), 0) + 1
    return count


SENDS = [sends(row) for row in range(Z)]
GROUPS = sorted(set().union(*SENDS))


def kernel(
    g_hbm, ids_hbm, logits_hbm, h_hbm, w_hbm, r_hbm,
    table_out, rn_out,
    held, ranks_of, wide_rows, slim_rows, prod, cross, hbuf, wbuf, acc, slot_acc, sent_scores,
    ids_v, logits_v, picked_v, st, rn, pk,
    load_sem, send_sem, recv_sem, cross_send, cross_recv,
    score_send, score_recv, r_send, r_recv, pk_send, pk_recv,
):
    sections = lax.axis_size("pp")
    s = lax.axis_index("pp")
    me = lax.axis_index("ep")
    core = lax.rem(me, CORES)
    chip = lax.div(me, CORES)
    x, z = lax.div(chip, Z), lax.rem(chip, Z)

    def at(xx, zz, cc=core):
        return (xx * Z + zz) * CORES + cc

    right, left = lax.rem(x + 1, X), lax.rem(x + X - 1, X)
    across = lax.rem(x + 2, X)
    sibling = (s, at(x, z, 1 - core))
    target = (
        (s, at(x, jnp.minimum(z + 1, Z - 1))),
        (s, at(x, jnp.maximum(z - 1, 0))),
        (s, at(right, z)),
        (s, at(left, z)),
    )
    opposite = (s, at(across, z))
    below = jnp.maximum(s - 1, 0)
    above = jnp.minimum(s + 1, sections - 1)

    def load(k, src, dst):
        return pltpu.make_async_copy(src, dst, load_sem.at[k])

    loads = [
        load(0, g_hbm, held.at[chip]),
        load(1, ids_hbm, ids_v),
        load(2, logits_hbm, logits_v),
        load(3, h_hbm.at[:, 1 - core], hbuf.at[0]),
        load(4, w_hbm.at[:, pl.ds(0, HALF)], wbuf.at[:, pl.ds(0, HALF)]),
        load(5, w_hbm.at[:, pl.ds(HALF, HALF)], wbuf.at[:, pl.ds(HALF, HALF)]),
        load(6, h_hbm.at[:, core], hbuf.at[1]),
    ]
    for copy in loads:
        copy.start()

    barrier = pltpu.get_barrier_semaphore()

    def greet(device):
        pl.semaphore_signal(barrier, inc=1, device_id=device, device_id_type=MESH)

    for device in (target[2], target[3], opposite, sibling):
        greet(device)

    @pl.when(z < Z - 1)
    def _():
        greet(target[0])

    @pl.when(z > 0)
    def _():
        greet(target[1])

    @pl.when(s < sections - 1)
    def _():
        @pl.loop(0, CHIPS)
        def _(q):
            greet((above, q * CORES + core))

    loads[1].wait()
    loads[2].wait()
    experts = lax.broadcasted_iota(jnp.int32, (EXPERTS, TOK), 0)
    ids = ids_v[...]
    named = jnp.zeros((EXPERTS, TOK), F32)
    for k in range(ids.shape[0]):
        named = named + (ids[k : k + 1] == experts).astype(F32)
    upper = (
        lax.broadcasted_iota(jnp.int32, (TOK, TOK), 0)
        < lax.broadcasted_iota(jnp.int32, (TOK, TOK), 1)
    ).astype(BF16)
    before = jnp.dot(named.astype(BF16), upper, preferred_element_type=F32)
    ranks = jnp.where(named > 0, before, -1.0).astype(BF16)
    ranks_of[chip] = jnp.concatenate([ranks[:RANK_ROWS], ranks[RANK_ROWS:]], axis=1)
    affinity = 1.0 / (1.0 + jnp.exp(-logits_v[...]))
    picked_v[...] = jnp.where(named > 0, affinity, 0.0)

    calls = 4 + (z < Z - 1).astype(jnp.int32) + (z > 0).astype(jnp.int32)
    calls = calls + CHIPS * (s > 0).astype(jnp.int32)
    pl.semaphore_wait(barrier, calls)

    def remote(src, dst, send, recv, device):
        return pltpu.make_async_remote_copy(
            src_ref=src, dst_ref=dst, send_sem=send, recv_sem=recv,
            device_id=device, device_id_type=MESH,
        )

    def lanes_of(piece):
        return pl.ds(OFFSET[piece], WIDTH[piece])

    def whole_ref(q, piece):
        if piece == RANKS:
            return ranks_of.at[q]
        return held.at[q, :, lanes_of(piece)]

    def rows_ref(q, piece):
        if piece < 2:
            own = lax.div(q, Z) == x
            place = 2 * lax.rem(q, Z) + jnp.where(own, 0, 1)
            return wide_rows.at[place, :, lanes_of(piece)]
        return slim_rows.at[q, :, pl.ds(OFFSET[piece] - OFFSET[2], WIDTH[piece])]

    def passing(way, q, piece):
        ref = whole_ref(q, piece)
        sent = send_sem.at[GROUPS.index((way, piece, WHOLE))]
        return remote(ref, ref, sent, recv_sem.at[q, piece], target[way])

    def passing_rows(way, q, piece):
        return remote(
            rows_ref(q, piece), held.at[q, pl.ds(0, BOTH), lanes_of(piece)],
            send_sem.at[GROUPS.index((way, piece, ROWS))], recv_sem.at[q, piece], target[way],
        )

    def chosen_rows(q, of):
        group = pl.ds(pl.multiple_of(lax.div(of * CORES, RANK_ROWS) * TOK, TOK), TOK)
        table = ranks_of[q, :, group].astype(F32)
        line = lax.broadcasted_iota(jnp.int32, (RANK_ROWS, TOK), 0)
        slot = lax.broadcasted_iota(jnp.int32, (MOST, TOK), 0).astype(F32)
        first = lax.rem(of * CORES, RANK_ROWS)
        hits = []
        for e in range(CORES):
            rank = jnp.sum(jnp.where(line == first + e, table, 0.0), axis=0, keepdims=True)
            hits.append(slot == rank)
        return hits

    neighbours = (chip + 1, chip - 1, right * Z + z, left * Z + z)

    def pass_on(q, piece):
        whole, some = goes(piece, x, z, lax.div(q, Z), lax.rem(q, Z))
        for way in range(4):
            if (way, piece, WHOLE) in GROUPS:

                @pl.when(whole[way])
                def _(way=way):
                    passing(way, q, piece).start()

        if piece == RANKS:
            return
        of, any_rows = chip, z < 0
        for way in range(4):
            of = jnp.where(some[way], neighbours[way], of)
            any_rows = any_rows | some[way]

        @pl.when(any_rows)
        def _():
            pick = jnp.concatenate([hit.astype(F32) for hit in chosen_rows(q, of)], axis=0)
            rows = jnp.dot(
                pick.astype(BF16), held[q, :, lanes_of(piece)], preferred_element_type=F32
            )
            rows_ref(q, piece)[...] = rows.astype(BF16)
            for way in range(4):
                if (way, piece, ROWS) in GROUPS:

                    @pl.when(some[way])
                    def _(way=way):
                        passing_rows(way, q, piece).start()

    rows = pl.ds(pl.multiple_of(core * RANK_ROWS, RANK_ROWS), RANK_ROWS)

    def quarter(xx):
        return pl.ds(pl.multiple_of(xx * QUARTER, 128), QUARTER)

    router_down = remote(
        r_hbm.at[rows, quarter(x)], rn.at[rows, quarter(x)], r_send.at[0], r_recv.at[0], (below, me)
    )

    @pl.when(s > 0)
    def _():
        router_down.start()

    pass_on(chip, RANKS)
    loads[0].wait()
    for piece in (3, 0, 1, 2):
        pass_on(chip, piece)
    picked_down = remote(picked_v, pk, pk_send, pk_recv, (below, me))

    @pl.when(s > 0)
    def _():
        picked_down.start()

    steps = [by_row(z, words) for words in zip(*map(packed, STEPS))]
    early = [by_row(z, words) for words in zip(*(packed(row[:EARLY]) for row in ORDER))]

    def outputs(which, half, store):
        lhs = hbuf[which].reshape(CHIPS * MOST, FFW)

        @pl.loop(0, HALF // 256)
        def _(t):
            cols = pl.ds(pl.multiple_of(half * HALF + t * 256, 256), 256)
            out = jnp.dot(lhs, wbuf[:, cols], preferred_element_type=F32)
            store(cols, out.astype(BF16).reshape(CHIPS, MOST, 256))

    def store_cross(cols, value):
        cross[:, :, cols] = value

    def store_own(cols, value):
        prod[:, core, :, cols] = value

    def crossing(half):
        cols = pl.ds(half * HALF, HALF)
        return remote(
            cross.at[:, :, cols], prod.at[:, core, :, cols],
            cross_send.at[half], cross_recv.at[half], sibling,
        )

    loads[3].wait()
    for half in range(2):
        loads[4 + half].wait()
        outputs(0, half, store_cross)
        crossing(half).start()
    loads[6].wait()
    for half in range(2):
        outputs(1, half, store_own)

    def arrived(q, piece, ref):
        remote(ref, ref, send_sem.at[0], recv_sem.at[q, piece], target[RIGHT]).wait_recv()

    def take(q, piece):
        if piece == RANKS:
            arrived(q, piece, ranks_of.at[q])
        else:
            full = arrives_whole(piece, x, z, lax.div(q, Z), lax.rem(q, Z))

            @pl.when(full)
            def _():
                arrived(q, piece, held.at[q, :, lanes_of(piece)])

            @pl.when(jnp.logical_not(full))
            def _():
                arrived(q, piece, held.at[q, pl.ds(0, BOTH), lanes_of(piece)])

        pass_on(q, piece)

    def decode(code):
        shard = lax.rem(code, 128)
        xo = lax.rem(x + lax.div(shard, 32), X)
        zo = lax.rem(lax.div(shard, 8), Z)
        return xo * Z + zo, lax.rem(shard, 8)

    def by_piece(piece, act):
        for k in range(5):

            @pl.when(piece == k)
            def _(k=k):
                act(k)

    @pl.loop(0, EARLY)
    def _(i):
        q, piece = decode(entry(early, i))
        by_piece(piece, functools.partial(take, q))

    def spread(k, device):
        ref = rn.at[rows, quarter(x)]
        return remote(ref, ref, r_send.at[1 + k], r_recv.at[1 + k], device)

    def came(k, xx):
        ref = rn.at[rows, quarter(xx)]
        return remote(ref, ref, r_send.at[1 + k], r_recv.at[1 + k], target[2])

    spreads = [spread(0, target[2]), spread(1, target[3]), spread(2, opposite)]
    own_rows = remote(rn.at[rows], rn.at[rows], r_send.at[4], r_recv.at[4], sibling)
    other = pl.ds(pl.multiple_of((1 - core) * RANK_ROWS, RANK_ROWS), RANK_ROWS)
    other_rows = remote(rn.at[other], rn.at[other], r_send.at[4], r_recv.at[4], sibling)

    @pl.when(s < sections - 1)
    def _():
        router_down.wait_recv()
        for copy in spreads:
            copy.start()

    for half in range(2):
        crossing(half).wait_recv()
    acc[...] = jnp.zeros_like(acc)
    slot_acc[...] = jnp.zeros_like(slot_acc)

    def score_copy(q):
        return remote(
            sent_scores.at[q], st.at[chip], score_send, score_recv,
            (below, q * CORES + core),
        )

    def score(q, piece):
        cols, width = lanes_of(piece), WIDTH[piece]
        full = arrives_whole(piece, x, z, lax.div(q, Z), lax.rem(q, Z))

        @pl.when(full)
        def _():
            acc[q] += lax.dot_general(
                prod[q, :, :, cols].reshape(BOTH, width), held[q, :, cols],
                (((1,), (1,)), ((), ())), preferred_element_type=F32,
            )

        @pl.when(jnp.logical_not(full))
        def _():
            terms = prod[q, :, :, cols].reshape(BOTH, width).astype(F32)
            terms = terms * held[q, :BOTH, cols].astype(F32)
            total = slot_acc[q]
            for k in range(0, width, TOK):
                total = total + terms[:, k : k + TOK]
            slot_acc[q] = total

    def finish(q):
        total = acc[q] + jnp.sum(slot_acc[q], axis=1, keepdims=True)
        lines = []
        for e, hit in enumerate(chosen_rows(q, chip)):
            part = total[e * MOST : (e + 1) * MOST]
            lines.append(jnp.sum(jnp.where(hit, part, 0.0), axis=0, keepdims=True))
        sent_scores[q] = jnp.concatenate(lines, axis=0)

        @pl.when(s > 0)
        def _():
            score_copy(q).start()

    @pl.loop(0, COUNT)
    def _(i):
        code = entry(steps, i)
        q, piece = decode(code)
        new = lax.rem(lax.div(code, 128), 2) == 1

        def step(k):
            @pl.when(new)
            def _():
                take(q, k)

            if k != RANKS:
                score(q, k)

        by_piece(piece, step)

        @pl.when(code >= 256)
        def _():
            finish(q)

        @pl.when((i == COUNT // 2) & (s < sections - 1))
        def _():
            came(0, left).wait_recv()
            came(1, right).wait_recv()
            came(2, across).wait_recv()
            own_rows.start()

    @pl.when(s < sections - 1)
    def _():
        other_rows.wait_recv()
        rn_out[...] = rn[...]
        picked_down.wait_recv()

        remote(sent_scores, st, score_send, score_recv, (below, me)).wait_recv()
        picked = pk[...]
        score_grad = jnp.concatenate([st[q] for q in range(CHIPS)], axis=0)
        picked_sum = jnp.sum(picked, axis=0, keepdims=True)
        mean_grad = jnp.sum(picked / picked_sum * score_grad, axis=0, keepdims=True)
        table = (score_grad - mean_grad) / picked_sum * picked * (1.0 - picked)
        square = jnp.concatenate([table, jnp.zeros((TOK - EXPERTS, TOK), F32)], axis=0)
        table_out[...] = square.T[:, :EXPERTS].astype(BF16)

    @pl.when(s == sections - 1)
    def _():
        rn_out[...] = jnp.zeros_like(rn_out)
        table_out[...] = jnp.zeros_like(table_out)

    for half in range(2):
        crossing(half).wait_send()

    @pl.when(s < sections - 1)
    def _():
        for copy in spreads:
            copy.wait_send()
        own_rows.wait_send()

    @pl.when(s > 0)
    def _():
        router_down.wait_send()
        picked_down.wait_send()
        remote(sent_scores, st, score_send, score_recv, (below, me)).wait_send()

    for row in range(Z):

        @pl.when(z == row)
        def _(row=row):
            for (way, piece, form), n in SENDS[row].items():
                if piece == RANKS:
                    ref = ranks_of.at[pl.ds(0, n)]
                else:
                    ref = held.at[pl.ds(0, n), pl.ds(0, (TOK, BOTH)[form]), lanes_of(piece)]
                sent = send_sem.at[GROUPS.index((way, piece, form))]
                remote(ref, ref, sent, recv_sem.at[0, 0], target[RIGHT]).wait_send()


def exchange(g, ids, logits, h, w, r):
    vmem = pl.BlockSpec(memory_space=pltpu.VMEM)
    dma = pltpu.SemaphoreType.DMA
    return pl.pallas_call(
        kernel,
        out_shape=(
            jax.ShapeDtypeStruct((TOK, EXPERTS), BF16),
            jax.ShapeDtypeStruct((EXPERTS, D), BF16),
        ),
        in_specs=[pl.BlockSpec(memory_space=pl.ANY)] * 6,
        out_specs=(vmem,) * 2,
        scratch_shapes=[
            pltpu.VMEM((CHIPS, TOK, D), BF16),
            pltpu.VMEM((CHIPS, RANK_ROWS, RANK_LANES), BF16),
            pltpu.VMEM((2 * Z, BOTH, OFFSET[2]), BF16),
            pltpu.VMEM((CHIPS, BOTH, D - OFFSET[2]), BF16),
            pltpu.VMEM((CHIPS, CORES, MOST, D), BF16),
            pltpu.VMEM((CHIPS, MOST, D), BF16),
            pltpu.VMEM((CORES, CHIPS, MOST, FFW), BF16),
            pltpu.VMEM((FFW, D), BF16),
            pltpu.VMEM((CHIPS, BOTH, TOK), F32),
            pltpu.VMEM((CHIPS, BOTH, TOK), F32),
            pltpu.VMEM((CHIPS, CORES, TOK), F32),
            pltpu.VMEM(ids.shape, jnp.int32),
            pltpu.VMEM(logits.shape, F32),
            pltpu.VMEM((EXPERTS, TOK), F32),
            pltpu.VMEM((CHIPS, CORES, TOK), F32),
            pltpu.VMEM((EXPERTS, D), BF16),
            pltpu.VMEM((EXPERTS, TOK), F32),
            dma((7,)),
            dma((len(GROUPS),)),
            dma((CHIPS, 5)),
            dma((2,)),
            dma((2,)),
            dma,
            dma,
            dma((5,)),
            dma((5,)),
            dma,
            dma,
        ],
        compiler_params=pltpu.CompilerParams(
            collective_id=0, has_side_effects=True, vmem_limit_bytes=52 * 2**20
        ),
    )(*(pltpu.with_memory_space_constraint(v, pltpu.HBM) for v in (g, ids, logits, h, w, r)))


def on_device(out_grads, expert_ids, router_logits, hidden_acts, w_down, w_router):
    h = hidden_acts.reshape(CHIPS, CORES, MOST, FFW)
    table, router = exchange(
        out_grads[0], expert_ids[0].T, router_logits[0].T, h, w_down[0, 0], w_router[0]
    )
    return jnp.dot(table, router, preferred_element_type=F32).astype(BF16)[None]


def solution(mesh):
    in_specs = (
        P("pp", "ep", None),
        P("pp", "ep", None),
        P("pp", "ep", None),
        P("pp", "ep", None, None),
        P("pp", "ep", None, None),
        P("pp", None, None),
    )
    out_specs = P("pp", "ep", None)
    return jax.shard_map(
        on_device, mesh=mesh, in_specs=in_specs, out_specs=out_specs, check_vma=False
    )
```

```python
import functools

import jax
import jax.numpy as jnp
from jax import lax
from jax.experimental import pallas as pl
from jax.experimental.pallas import tpu as pltpu
from jax.sharding import PartitionSpec as P

MESH = pl.DeviceIdType.MESH
F32, BF16 = jnp.float32, jnp.bfloat16

X, Z, CORES = 4, 4, 2
CHIPS = X * Z
TOK, D, FFW, MOST, EXPERTS = 128, 3584, 1024, 48, 32
BOTH = CORES * MOST
WIDTH = (1408, 1408, 384, 384)
OFFSET = (0, 1408, 2816, 3200)
RANKS = 4
RANK_ROWS, RANK_LANES = 16, 256
QUARTER = D // X
HALF = D // 2

ORDER = (
    (
        12, 36, 100, 10, 34, 98, 97, 9, 33, 32, 96, 8, 35, 99, 44, 108, 68, 11, 20, 66, 18, 42, 106, 105, 41,
        17, 65, 64, 40, 16, 104, 67, 116, 76, 52, 43, 107, 19, 28, 113, 74, 73, 26, 50, 114, 112, 49, 25, 72, 124,
        48, 84, 60, 80, 81, 24, 51, 115, 27, 121, 75, 57, 92, 82, 58, 122, 120, 59, 56, 123, 83, 90, 91, 89, 88,
    ),
    (
        4, 20, 44, 108, 2, 18, 42, 106, 105, 1, 17, 41, 40, 104, 0, 16, 43, 107, 36, 100, 52, 116, 76, 3, 19,
        28, 74, 34, 26, 98, 50, 33, 97, 35, 114, 99, 66, 113, 49, 25, 72, 73, 24, 67, 51, 32, 96, 115, 27, 48,
        112, 75, 124, 68, 84, 82, 60, 58, 122, 59, 123, 121, 65, 83, 81, 120, 64, 57, 80, 56, 92, 90, 91, 88, 89,
    ),
    (
        12, 28, 52, 116, 10, 26, 50, 114, 113, 9, 25, 49, 48, 112, 8, 24, 51, 115, 44, 108, 60, 124, 84, 11, 27,
        4, 82, 58, 2, 122, 42, 41, 105, 59, 106, 123, 90, 121, 57, 1, 80, 81, 0, 91, 43, 40, 104, 107, 3, 56,
        120, 83, 100, 76, 74, 92, 36, 34, 98, 35, 99, 97, 73, 75, 89, 96, 72, 33, 88, 32, 68, 66, 67, 64, 65,
    ),
    (
        20, 60, 124, 18, 58, 122, 121, 17, 57, 56, 120, 16, 59, 123, 52, 116, 92, 19, 12, 90, 10, 50, 114, 113, 49,
        9, 89, 88, 48, 8, 112, 91, 108, 84, 44, 51, 115, 11, 4, 105, 82, 81, 2, 42, 106, 104, 41, 1, 80, 100,
        40, 76, 36, 72, 73, 0, 43, 107, 3, 97, 83, 33, 68, 74, 34, 98, 96, 35, 32, 99, 75, 66, 67, 65, 64,
    ),
)
EARLY = 14


def programme(z):
    late = [8 * z + p for p in range(4)] + [code for code in ORDER[z][:EARLY] if code % 8 != RANKS]
    steps = []
    for code in ORDER[z][EARLY:]:
        if late:
            steps.append(late.pop(0))
        steps.append(code + 128)
    left = {}
    for code in steps:
        left[code % 128 // 8] = left.get(code % 128 // 8, 0) + 1
    out = []
    for code in steps:
        shard = code % 128 // 8
        left[shard] -= 1
        out.append(code + (256 if left[shard] == 0 else 0))
    return out


STEPS = [programme(z) for z in range(Z)]
COUNT = max(map(len, STEPS))
IDLE = 5
STEPS = [steps + [IDLE] * (COUNT - len(steps)) for steps in STEPS]


def packed(codes):
    words = []
    for k in range(0, len(codes), 3):
        words.append(sum(code << (9 * j) for j, code in enumerate(codes[k : k + 3])))
    return words


def by_row(z, values):
    picked = jnp.int32(values[Z - 1])
    for row in range(Z - 1):
        picked = jnp.where(z == row, jnp.int32(values[row]), picked)
    return picked


def entry(words, i):
    place = lax.div(i, 3)
    while len(words) > 1:
        odd = lax.rem(place, 2) == 1
        halved = []
        for k in range(0, len(words), 2):
            more = k + 1 < len(words)
            halved.append(jnp.where(odd, words[k + 1], words[k]) if more else words[k])
        words, place = halved, lax.div(place, 2)
    turn = lax.rem(i, 3)
    scale = jnp.where(turn == 0, 1, jnp.where(turn == 1, 1 << 9, 1 << 18))
    return lax.rem(lax.div(words[0], scale), 512)


UP, DOWN, RIGHT, LEFT = range(4)
WHOLE, ROWS = range(2)


def rem(a, b):
    return a % b if isinstance(a, int) else lax.rem(a, b)


def goes(piece, x, z, xo, zo):
    dx = rem(xo - x + X, X)
    even = piece % 2 == 0
    up, down = (zo <= z) & (z < Z - 1), (zo >= z) & (z > 0)
    here = dx == 0
    beside = dx == (X - 1 if even else 1)
    no = z < 0
    if piece == RANKS:
        return (here & up, here & down, here, here | (dx == 1)), (no,) * 4
    if piece < 2:
        if even:
            return (here & up, here & down, here, no), (no, no, beside, here)
        return (here & up, here & down, no, here), (no, no, here, beside)
    row = zo == z
    across = (row & (here | beside), row & here)
    if not even:
        across = across[::-1]
    return (up & (z != Z - 2), down & (z != 1), *across), (up & (z == Z - 2), down & (z == 1), no, no)


def arrives_whole(piece, x, z, xo, zo):
    dx = rem(xo - x + X, X)
    if piece < 2:
        return (dx == 0) | (dx == (X - 1 if piece == 0 else 1))
    return (zo == z) | ((z > 0) & (z < Z - 1))


def sends(row):
    count = {}
    for q in range(CHIPS):
        for piece in range(5):
            for form, ways in enumerate(goes(piece, 0, row, q // Z, q % Z)):
                for way in range(4):
                    if ways[way]:
                        count[way, piece, form] = count.get((way, piece, form), 0) + 1
    return count


SENDS = [sends(row) for row in range(Z)]
GROUPS = sorted(set().union(*SENDS))


def kernel(
    g_hbm, ids_hbm, logits_hbm, h_hbm, w_hbm, r_hbm,
    table_out, rn_out,
    held, ranks_of, wide_rows, slim_rows, prod, cross, hbuf, wbuf, acc, slot_acc, sent_scores,
    ids_v, logits_v, picked_v, st, rn, pk,
    load_sem, send_sem, recv_sem, cross_send, cross_recv,
    score_send, score_recv, r_send, r_recv, pk_send, pk_recv,
):
    sections = lax.axis_size("pp")
    s = lax.axis_index("pp")
    me = lax.axis_index("ep")
    core = lax.rem(me, CORES)
    chip = lax.div(me, CORES)
    x, z = lax.div(chip, Z), lax.rem(chip, Z)

    def at(xx, zz, cc=core):
        return (xx * Z + zz) * CORES + cc

    right, left = lax.rem(x + 1, X), lax.rem(x + X - 1, X)
    across = lax.rem(x + 2, X)
    sibling = (s, at(x, z, 1 - core))
    target = (
        (s, at(x, jnp.minimum(z + 1, Z - 1))),
        (s, at(x, jnp.maximum(z - 1, 0))),
        (s, at(right, z)),
        (s, at(left, z)),
    )
    opposite = (s, at(across, z))
    below = jnp.maximum(s - 1, 0)
    above = jnp.minimum(s + 1, sections - 1)

    def load(k, src, dst):
        return pltpu.make_async_copy(src, dst, load_sem.at[k])

    loads = [
        load(0, g_hbm, held.at[chip]),
        load(1, ids_hbm, ids_v),
        load(2, logits_hbm, logits_v),
        load(3, h_hbm.at[:, 1 - core], hbuf.at[0]),
        load(4, w_hbm.at[:, pl.ds(0, HALF)], wbuf.at[:, pl.ds(0, HALF)]),
        load(5, w_hbm.at[:, pl.ds(HALF, HALF)], wbuf.at[:, pl.ds(HALF, HALF)]),
        load(6, h_hbm.at[:, core], hbuf.at[1]),
    ]
    for copy in loads[:3]:
        copy.start()

    barrier = pltpu.get_barrier_semaphore()

    def greet(device):
        pl.semaphore_signal(barrier, inc=1, device_id=device, device_id_type=MESH)

    for device in (target[2], target[3], opposite, sibling):
        greet(device)

    @pl.when(z < Z - 1)
    def _():
        greet(target[0])

    @pl.when(z > 0)
    def _():
        greet(target[1])

    @pl.when(s < sections - 1)
    def _():
        @pl.loop(0, CHIPS)
        def _(q):
            greet((above, q * CORES + core))

    for copy in loads[3:]:
        copy.start()

    loads[1].wait()
    loads[2].wait()
    experts = lax.broadcasted_iota(jnp.int32, (EXPERTS, TOK), 0)
    ids = ids_v[...]
    named = jnp.zeros((EXPERTS, TOK), F32)
    for k in range(ids.shape[0]):
        named = named + (ids[k : k + 1] == experts).astype(F32)
    upper = (
        lax.broadcasted_iota(jnp.int32, (TOK, TOK), 0)
        < lax.broadcasted_iota(jnp.int32, (TOK, TOK), 1)
    ).astype(BF16)
    before = jnp.dot(named.astype(BF16), upper, preferred_element_type=F32)
    ranks = jnp.where(named > 0, before, -1.0).astype(BF16)
    ranks_of[chip] = jnp.concatenate([ranks[:RANK_ROWS], ranks[RANK_ROWS:]], axis=1)
    affinity = 1.0 / (1.0 + jnp.exp(-logits_v[...]))
    picked_v[...] = jnp.where(named > 0, affinity, 0.0)

    calls = 4 + (z < Z - 1).astype(jnp.int32) + (z > 0).astype(jnp.int32)
    calls = calls + CHIPS * (s > 0).astype(jnp.int32)
    pl.semaphore_wait(barrier, calls)

    def remote(src, dst, send, recv, device):
        return pltpu.make_async_remote_copy(
            src_ref=src, dst_ref=dst, send_sem=send, recv_sem=recv,
            device_id=device, device_id_type=MESH,
        )

    def lanes_of(piece):
        return pl.ds(OFFSET[piece], WIDTH[piece])

    def whole_ref(q, piece):
        if piece == RANKS:
            return ranks_of.at[q]
        return held.at[q, :, lanes_of(piece)]

    def rows_ref(q, piece):
        if piece < 2:
            own = lax.div(q, Z) == x
            place = 2 * lax.rem(q, Z) + jnp.where(own, 0, 1)
            return wide_rows.at[place, :, lanes_of(piece)]
        return slim_rows.at[q, :, pl.ds(OFFSET[piece] - OFFSET[2], WIDTH[piece])]

    def passing(way, q, piece):
        ref = whole_ref(q, piece)
        sent = send_sem.at[GROUPS.index((way, piece, WHOLE))]
        return remote(ref, ref, sent, recv_sem.at[q, piece], target[way])

    def passing_rows(way, q, piece):
        return remote(
            rows_ref(q, piece), held.at[q, pl.ds(0, BOTH), lanes_of(piece)],
            send_sem.at[GROUPS.index((way, piece, ROWS))], recv_sem.at[q, piece], target[way],
        )

    def chosen_rows(q, of):
        group = pl.ds(pl.multiple_of(lax.div(of * CORES, RANK_ROWS) * TOK, TOK), TOK)
        table = ranks_of[q, :, group].astype(F32)
        line = lax.broadcasted_iota(jnp.int32, (RANK_ROWS, TOK), 0)
        slot = lax.broadcasted_iota(jnp.int32, (MOST, TOK), 0).astype(F32)
        first = lax.rem(of * CORES, RANK_ROWS)
        hits = []
        for e in range(CORES):
            rank = jnp.sum(jnp.where(line == first + e, table, 0.0), axis=0, keepdims=True)
            hits.append(slot == rank)
        return hits

    neighbours = (chip + 1, chip - 1, right * Z + z, left * Z + z)

    def pass_on(q, piece):
        whole, some = goes(piece, x, z, lax.div(q, Z), lax.rem(q, Z))
        for way in range(4):
            if (way, piece, WHOLE) in GROUPS:

                @pl.when(whole[way])
                def _(way=way):
                    passing(way, q, piece).start()

        if piece == RANKS:
            return
        of, any_rows = chip, z < 0
        for way in range(4):
            of = jnp.where(some[way], neighbours[way], of)
            any_rows = any_rows | some[way]

        @pl.when(any_rows)
        def _():
            pick = jnp.concatenate([hit.astype(F32) for hit in chosen_rows(q, of)], axis=0)
            rows = jnp.dot(
                pick.astype(BF16), held[q, :, lanes_of(piece)], preferred_element_type=F32
            )
            rows_ref(q, piece)[...] = rows.astype(BF16)
            for way in range(4):
                if (way, piece, ROWS) in GROUPS:

                    @pl.when(some[way])
                    def _(way=way):
                        passing_rows(way, q, piece).start()

    rows = pl.ds(pl.multiple_of(core * RANK_ROWS, RANK_ROWS), RANK_ROWS)

    def quarter(xx):
        return pl.ds(pl.multiple_of(xx * QUARTER, 128), QUARTER)

    router_down = remote(
        r_hbm.at[rows, quarter(x)], rn.at[rows, quarter(x)], r_send.at[0], r_recv.at[0], (below, me)
    )

    @pl.when(s > 0)
    def _():
        router_down.start()

    pass_on(chip, RANKS)
    loads[0].wait()
    for piece in (2, 1, 0, 3):
        pass_on(chip, piece)
    picked_down = remote(picked_v, pk, pk_send, pk_recv, (below, me))

    @pl.when(s > 0)
    def _():
        picked_down.start()

    steps = [by_row(z, words) for words in zip(*map(packed, STEPS))]
    early = [by_row(z, words) for words in zip(*(packed(row[:EARLY]) for row in ORDER))]

    def outputs(which, half, store):
        lhs = hbuf[which].reshape(CHIPS * MOST, FFW)

        @pl.loop(0, HALF // 256)
        def _(t):
            cols = pl.ds(pl.multiple_of(half * HALF + t * 256, 256), 256)
            out = jnp.dot(lhs, wbuf[:, cols], preferred_element_type=F32)
            store(cols, out.astype(BF16).reshape(CHIPS, MOST, 256))

    def store_cross(cols, value):
        cross[:, :, cols] = value

    def store_own(cols, value):
        prod[:, core, :, cols] = value

    def crossing(half):
        cols = pl.ds(half * HALF, HALF)
        return remote(
            cross.at[:, :, cols], prod.at[:, core, :, cols],
            cross_send.at[half], cross_recv.at[half], sibling,
        )

    loads[3].wait()
    for half in range(2):
        loads[4 + half].wait()
        outputs(0, half, store_cross)
        crossing(half).start()
    loads[6].wait()
    for half in range(2):
        outputs(1, half, store_own)

    def arrived(q, piece, ref):
        remote(ref, ref, send_sem.at[0], recv_sem.at[q, piece], target[RIGHT]).wait_recv()

    def take(q, piece):
        if piece == RANKS:
            arrived(q, piece, ranks_of.at[q])
        else:
            full = arrives_whole(piece, x, z, lax.div(q, Z), lax.rem(q, Z))

            @pl.when(full)
            def _():
                arrived(q, piece, held.at[q, :, lanes_of(piece)])

            @pl.when(jnp.logical_not(full))
            def _():
                arrived(q, piece, held.at[q, pl.ds(0, BOTH), lanes_of(piece)])

        pass_on(q, piece)

    def decode(code):
        shard = lax.rem(code, 128)
        xo = lax.rem(x + lax.div(shard, 32), X)
        zo = lax.rem(lax.div(shard, 8), Z)
        return xo * Z + zo, lax.rem(shard, 8)

    def by_piece(piece, act):
        for k in range(5):

            @pl.when(piece == k)
            def _(k=k):
                act(k)

    @pl.loop(0, EARLY)
    def _(i):
        q, piece = decode(entry(early, i))
        by_piece(piece, functools.partial(take, q))

    def spread(k, device):
        ref = rn.at[rows, quarter(x)]
        return remote(ref, ref, r_send.at[1 + k], r_recv.at[1 + k], device)

    def came(k, xx):
        ref = rn.at[rows, quarter(xx)]
        return remote(ref, ref, r_send.at[1 + k], r_recv.at[1 + k], target[2])

    spreads = [spread(0, target[2]), spread(1, target[3]), spread(2, opposite)]
    own_rows = remote(rn.at[rows], rn.at[rows], r_send.at[4], r_recv.at[4], sibling)
    other = pl.ds(pl.multiple_of((1 - core) * RANK_ROWS, RANK_ROWS), RANK_ROWS)
    other_rows = remote(rn.at[other], rn.at[other], r_send.at[4], r_recv.at[4], sibling)

    for half in range(2):
        crossing(half).wait_recv()
    acc[...] = jnp.zeros_like(acc)
    slot_acc[...] = jnp.zeros_like(slot_acc)

    def score_copy(q):
        return remote(
            sent_scores.at[q], st.at[chip], score_send, score_recv,
            (below, q * CORES + core),
        )

    def score(q, piece):
        cols, width = lanes_of(piece), WIDTH[piece]
        full = arrives_whole(piece, x, z, lax.div(q, Z), lax.rem(q, Z))

        @pl.when(full)
        def _():
            acc[q] += lax.dot_general(
                prod[q, :, :, cols].reshape(BOTH, width), held[q, :, cols],
                (((1,), (1,)), ((), ())), preferred_element_type=F32,
            )

        @pl.when(jnp.logical_not(full))
        def _():
            terms = prod[q, :, :, cols].reshape(BOTH, width).astype(F32)
            terms = terms * held[q, :BOTH, cols].astype(F32)
            total = slot_acc[q]
            for k in range(0, width, TOK):
                total = total + terms[:, k : k + TOK]
            slot_acc[q] = total

    def finish(q):
        total = acc[q] + jnp.sum(slot_acc[q], axis=1, keepdims=True)
        lines = []
        for e, hit in enumerate(chosen_rows(q, chip)):
            part = total[e * MOST : (e + 1) * MOST]
            lines.append(jnp.sum(jnp.where(hit, part, 0.0), axis=0, keepdims=True))
        sent_scores[q] = jnp.concatenate(lines, axis=0)

        @pl.when(s > 0)
        def _():
            score_copy(q).start()

    @pl.loop(0, COUNT)
    def _(i):
        code = entry(steps, i)
        q, piece = decode(code)
        new = lax.rem(lax.div(code, 128), 2) == 1

        def step(k):
            @pl.when(new)
            def _():
                take(q, k)

            if k != RANKS:
                score(q, k)

        by_piece(piece, step)

        @pl.when(code >= 256)
        def _():
            finish(q)

        @pl.when((i == COUNT // 4) & (s < sections - 1))
        def _():
            router_down.wait_recv()
            for copy in spreads:
                copy.start()

        @pl.when((i == 3 * COUNT // 4) & (s < sections - 1))
        def _():
            came(0, left).wait_recv()
            came(1, right).wait_recv()
            came(2, across).wait_recv()
            own_rows.start()

    @pl.when(s < sections - 1)
    def _():
        other_rows.wait_recv()
        rn_out[...] = rn[...]
        picked_down.wait_recv()
        picked = pk[...]
        weight = picked / jnp.sum(picked, axis=0, keepdims=True)
        slope = weight * (1.0 - picked)
        remote(sent_scores, st, score_send, score_recv, (below, me)).wait_recv()
        score_grad = jnp.concatenate([st[q] for q in range(CHIPS)], axis=0)
        mean_grad = jnp.sum(weight * score_grad, axis=0, keepdims=True)
        table = (score_grad - mean_grad) * slope
        square = jnp.concatenate([table, jnp.zeros((TOK - EXPERTS, TOK), F32)], axis=0)
        table_out[...] = square.T[:, :EXPERTS].astype(BF16)

    @pl.when(s == sections - 1)
    def _():
        rn_out[...] = jnp.zeros_like(rn_out)
        table_out[...] = jnp.zeros_like(table_out)

    for half in range(2):
        crossing(half).wait_send()

    @pl.when(s < sections - 1)
    def _():
        for copy in spreads:
            copy.wait_send()
        own_rows.wait_send()

    @pl.when(s > 0)
    def _():
        router_down.wait_send()
        picked_down.wait_send()
        remote(sent_scores, st, score_send, score_recv, (below, me)).wait_send()

    for row in range(Z):

        @pl.when(z == row)
        def _(row=row):
            for (way, piece, form), n in SENDS[row].items():
                if piece == RANKS:
                    ref = ranks_of.at[pl.ds(0, n)]
                else:
                    ref = held.at[pl.ds(0, n), pl.ds(0, (TOK, BOTH)[form]), lanes_of(piece)]
                sent = send_sem.at[GROUPS.index((way, piece, form))]
                remote(ref, ref, sent, recv_sem.at[0, 0], target[RIGHT]).wait_send()


def exchange(g, ids, logits, h, w, r):
    vmem = pl.BlockSpec(memory_space=pltpu.VMEM)
    dma = pltpu.SemaphoreType.DMA
    return pl.pallas_call(
        kernel,
        out_shape=(
            jax.ShapeDtypeStruct((TOK, EXPERTS), BF16),
            jax.ShapeDtypeStruct((EXPERTS, D), BF16),
        ),
        in_specs=[pl.BlockSpec(memory_space=pl.ANY)] * 6,
        out_specs=(vmem,) * 2,
        scratch_shapes=[
            pltpu.VMEM((CHIPS, TOK, D), BF16),
            pltpu.VMEM((CHIPS, RANK_ROWS, RANK_LANES), BF16),
            pltpu.VMEM((2 * Z, BOTH, OFFSET[2]), BF16),
            pltpu.VMEM((CHIPS, BOTH, D - OFFSET[2]), BF16),
            pltpu.VMEM((CHIPS, CORES, MOST, D), BF16),
            pltpu.VMEM((CHIPS, MOST, D), BF16),
            pltpu.VMEM((CORES, CHIPS, MOST, FFW), BF16),
            pltpu.VMEM((FFW, D), BF16),
            pltpu.VMEM((CHIPS, BOTH, TOK), F32),
            pltpu.VMEM((CHIPS, BOTH, TOK), F32),
            pltpu.VMEM((CHIPS, CORES, TOK), F32),
            pltpu.VMEM(ids.shape, jnp.int32),
            pltpu.VMEM(logits.shape, F32),
            pltpu.VMEM((EXPERTS, TOK), F32),
            pltpu.VMEM((CHIPS, CORES, TOK), F32),
            pltpu.VMEM((EXPERTS, D), BF16),
            pltpu.VMEM((EXPERTS, TOK), F32),
            dma((7,)),
            dma((len(GROUPS),)),
            dma((CHIPS, 5)),
            dma((2,)),
            dma((2,)),
            dma,
            dma,
            dma((5,)),
            dma((5,)),
            dma,
            dma,
        ],
        compiler_params=pltpu.CompilerParams(
            collective_id=0, has_side_effects=True, vmem_limit_bytes=52 * 2**20
        ),
    )(*(pltpu.with_memory_space_constraint(v, pltpu.HBM) for v in (g, ids, logits, h, w, r)))


def on_device(out_grads, expert_ids, router_logits, hidden_acts, w_down, w_router):
    h = hidden_acts.reshape(CHIPS, CORES, MOST, FFW)
    table, router = exchange(
        out_grads[0], expert_ids[0].T, router_logits[0].T, h, w_down[0, 0], w_router[0]
    )
    return jnp.dot(table, router, preferred_element_type=F32).astype(BF16)[None]


def solution(mesh):
    in_specs = (
        P("pp", "ep", None),
        P("pp", "ep", None),
        P("pp", "ep", None),
        P("pp", "ep", None, None),
        P("pp", "ep", None, None),
        P("pp", None, None),
    )
    out_specs = P("pp", "ep", None)
    return jax.shard_map(
        on_device, mesh=mesh, in_specs=in_specs, out_specs=out_specs, check_vma=False
    )
```

```python
import functools

import jax
import jax.numpy as jnp
from jax import lax
from jax.experimental import pallas as pl
from jax.experimental.pallas import tpu as pltpu
from jax.sharding import PartitionSpec as P

MESH = pl.DeviceIdType.MESH
F32, BF16 = jnp.float32, jnp.bfloat16

X, Z, CORES = 4, 4, 2
CHIPS = X * Z
TOK, D, FFW, MOST, EXPERTS = 128, 3584, 1024, 48, 32
BOTH = CORES * MOST
WIDTH = (1408, 1408, 384, 384)
OFFSET = (0, 1408, 2816, 3200)
RANKS = 4
RANK_ROWS, RANK_LANES = 16, 256
QUARTER = D // X
HALF = D // 2

ORDER = (
    (
        12, 36, 100, 10, 34, 98, 97, 9, 33, 32, 96, 8, 35, 99, 44, 108, 68, 11, 20, 66, 18, 42, 106, 105, 41,
        17, 65, 64, 40, 16, 104, 67, 116, 76, 52, 43, 107, 19, 28, 113, 74, 73, 26, 50, 114, 112, 49, 25, 72, 124,
        48, 84, 60, 80, 81, 24, 51, 115, 27, 121, 75, 57, 92, 82, 58, 122, 120, 59, 56, 123, 83, 90, 91, 89, 88,
    ),
    (
        4, 20, 44, 108, 2, 18, 42, 106, 105, 1, 17, 41, 40, 104, 0, 16, 43, 107, 36, 100, 52, 116, 76, 3, 19,
        28, 74, 34, 26, 98, 50, 33, 97, 35, 114, 99, 66, 113, 49, 25, 72, 73, 24, 67, 51, 32, 96, 115, 27, 48,
        112, 75, 124, 68, 84, 82, 60, 58, 122, 59, 123, 121, 65, 83, 81, 120, 64, 57, 80, 56, 92, 90, 91, 88, 89,
    ),
    (
        12, 28, 52, 116, 10, 26, 50, 114, 113, 9, 25, 49, 48, 112, 8, 24, 51, 115, 44, 108, 60, 124, 84, 11, 27,
        4, 82, 58, 2, 122, 42, 41, 105, 59, 106, 123, 90, 121, 57, 1, 80, 81, 0, 91, 43, 40, 104, 107, 3, 56,
        120, 83, 100, 76, 74, 92, 36, 34, 98, 35, 99, 97, 73, 75, 89, 96, 72, 33, 88, 32, 68, 66, 67, 64, 65,
    ),
    (
        20, 60, 124, 18, 58, 122, 121, 17, 57, 56, 120, 16, 59, 123, 52, 116, 92, 19, 12, 90, 10, 50, 114, 113, 49,
        9, 89, 88, 48, 8, 112, 91, 108, 84, 44, 51, 115, 11, 4, 105, 82, 81, 2, 42, 106, 104, 41, 1, 80, 100,
        40, 76, 36, 72, 73, 0, 43, 107, 3, 97, 83, 33, 68, 74, 34, 98, 96, 35, 32, 99, 75, 66, 67, 65, 64,
    ),
)
EARLY = 14


def programme(z):
    late = [8 * z + p for p in range(4)] + [code for code in ORDER[z][:EARLY] if code % 8 != RANKS]
    steps = []
    for code in ORDER[z][EARLY:]:
        if late:
            steps.append(late.pop(0))
        steps.append(code + 128)
    left = {}
    for code in steps:
        left[code % 128 // 8] = left.get(code % 128 // 8, 0) + 1
    out = []
    for code in steps:
        shard = code % 128 // 8
        left[shard] -= 1
        out.append(code + (256 if left[shard] == 0 else 0))
    return out


STEPS = [programme(z) for z in range(Z)]
COUNT = max(map(len, STEPS))
IDLE = 5
STEPS = [steps + [IDLE] * (COUNT - len(steps)) for steps in STEPS]


def packed(codes):
    words = []
    for k in range(0, len(codes), 3):
        words.append(sum(code << (9 * j) for j, code in enumerate(codes[k : k + 3])))
    return words


def by_row(z, values):
    picked = jnp.int32(values[Z - 1])
    for row in range(Z - 1):
        picked = jnp.where(z == row, jnp.int32(values[row]), picked)
    return picked


def entry(words, i):
    place = lax.div(i, 3)
    while len(words) > 1:
        odd = lax.rem(place, 2) == 1
        halved = []
        for k in range(0, len(words), 2):
            more = k + 1 < len(words)
            halved.append(jnp.where(odd, words[k + 1], words[k]) if more else words[k])
        words, place = halved, lax.div(place, 2)
    turn = lax.rem(i, 3)
    scale = jnp.where(turn == 0, 1, jnp.where(turn == 1, 1 << 9, 1 << 18))
    return lax.rem(lax.div(words[0], scale), 512)


UP, DOWN, RIGHT, LEFT = range(4)
WHOLE, ROWS = range(2)


def rem(a, b):
    return a % b if isinstance(a, int) else lax.rem(a, b)


def goes(piece, x, z, xo, zo):
    dx = rem(xo - x + X, X)
    even = piece % 2 == 0
    up, down = (zo <= z) & (z < Z - 1), (zo >= z) & (z > 0)
    here = dx == 0
    beside = dx == (X - 1 if even else 1)
    no = z < 0
    if piece == RANKS:
        return (here & up, here & down, here, here | (dx == 1)), (no,) * 4
    if piece < 2:
        if even:
            return (here & up, here & down, here, no), (no, no, beside, here)
        return (here & up, here & down, no, here), (no, no, here, beside)
    row = zo == z
    across = (row & (here | beside), row & here)
    if not even:
        across = across[::-1]
    return (up & (z != Z - 2), down & (z != 1), *across), (up & (z == Z - 2), down & (z == 1), no, no)


def arrives_whole(piece, x, z, xo, zo):
    dx = rem(xo - x + X, X)
    if piece < 2:
        return (dx == 0) | (dx == (X - 1 if piece == 0 else 1))
    return (zo == z) | ((z > 0) & (z < Z - 1))


def sends(row):
    count = {}
    for q in range(CHIPS):
        for piece in range(5):
            for form, ways in enumerate(goes(piece, 0, row, q // Z, q % Z)):
                for way in range(4):
                    if ways[way]:
                        count[way, piece, form] = count.get((way, piece, form), 0) + 1
    return count


SENDS = [sends(row) for row in range(Z)]
GROUPS = sorted(set().union(*SENDS))


def kernel(
    g_hbm, ids_hbm, logits_hbm, h_hbm, w_hbm, r_hbm,
    table_out, rn_out,
    held, ranks_of, wide_rows, slim_rows, prod, cross, hbuf, wbuf, acc, slot_acc, sent_scores,
    ids_v, logits_v, picked_v, st, rn, pk, next_ids,
    load_sem, send_sem, recv_sem, cross_send, cross_recv,
    score_send, score_recv, r_send, r_recv, pk_send, pk_recv, ids_send, ids_recv,
):
    sections = lax.axis_size("pp")
    s = lax.axis_index("pp")
    me = lax.axis_index("ep")
    core = lax.rem(me, CORES)
    chip = lax.div(me, CORES)
    x, z = lax.div(chip, Z), lax.rem(chip, Z)

    def at(xx, zz, cc=core):
        return (xx * Z + zz) * CORES + cc

    right, left = lax.rem(x + 1, X), lax.rem(x + X - 1, X)
    across = lax.rem(x + 2, X)
    sibling = (s, at(x, z, 1 - core))
    target = (
        (s, at(x, jnp.minimum(z + 1, Z - 1))),
        (s, at(x, jnp.maximum(z - 1, 0))),
        (s, at(right, z)),
        (s, at(left, z)),
    )
    opposite = (s, at(across, z))
    below = jnp.maximum(s - 1, 0)
    above = jnp.minimum(s + 1, sections - 1)

    def load(k, src, dst):
        return pltpu.make_async_copy(src, dst, load_sem.at[k])

    loads = [
        load(0, g_hbm, held.at[chip]),
        load(1, ids_hbm, ids_v),
        load(2, logits_hbm, logits_v),
        load(3, h_hbm.at[:, 1 - core], hbuf.at[0]),
        load(4, w_hbm.at[:, pl.ds(0, HALF)], wbuf.at[:, pl.ds(0, HALF)]),
        load(5, w_hbm.at[:, pl.ds(HALF, HALF)], wbuf.at[:, pl.ds(HALF, HALF)]),
        load(6, h_hbm.at[:, core], hbuf.at[1]),
    ]
    for copy in loads[:3]:
        copy.start()

    barrier = pltpu.get_barrier_semaphore()

    def greet(device):
        pl.semaphore_signal(barrier, inc=1, device_id=device, device_id_type=MESH)

    for device in (target[2], target[3], opposite, sibling):
        greet(device)

    @pl.when(z < Z - 1)
    def _():
        greet(target[0])

    @pl.when(z > 0)
    def _():
        greet(target[1])

    @pl.when(s < sections - 1)
    def _():
        @pl.loop(0, CHIPS)
        def _(q):
            greet((above, q * CORES + core))

    for copy in loads[3:]:
        copy.start()

    loads[1].wait()
    loads[2].wait()
    experts = lax.broadcasted_iota(jnp.int32, (EXPERTS, TOK), 0)
    ids = ids_v[...]
    named = jnp.zeros((EXPERTS, TOK), F32)
    for k in range(ids.shape[0]):
        named = named + (ids[k : k + 1] == experts).astype(F32)
    upper = (
        lax.broadcasted_iota(jnp.int32, (TOK, TOK), 0)
        < lax.broadcasted_iota(jnp.int32, (TOK, TOK), 1)
    ).astype(BF16)
    before = jnp.dot(named.astype(BF16), upper, preferred_element_type=F32)
    ranks = jnp.where(named > 0, before, -1.0).astype(BF16)
    ranks_of[chip] = jnp.concatenate([ranks[:RANK_ROWS], ranks[RANK_ROWS:]], axis=1)
    affinity = 1.0 / (1.0 + jnp.exp(-logits_v[...]))
    for k in range(ids.shape[0]):
        mine = jnp.where(ids[k : k + 1] == experts, affinity, 0.0)
        picked_v[k : k + 1, :] = jnp.sum(mine, axis=0, keepdims=True)

    calls = 4 + (z < Z - 1).astype(jnp.int32) + (z > 0).astype(jnp.int32)
    calls = calls + CHIPS * (s > 0).astype(jnp.int32)
    pl.semaphore_wait(barrier, calls)

    def remote(src, dst, send, recv, device):
        return pltpu.make_async_remote_copy(
            src_ref=src, dst_ref=dst, send_sem=send, recv_sem=recv,
            device_id=device, device_id_type=MESH,
        )

    def lanes_of(piece):
        return pl.ds(OFFSET[piece], WIDTH[piece])

    def whole_ref(q, piece):
        if piece == RANKS:
            return ranks_of.at[q]
        return held.at[q, :, lanes_of(piece)]

    def rows_ref(q, piece):
        if piece < 2:
            own = lax.div(q, Z) == x
            place = 2 * lax.rem(q, Z) + jnp.where(own, 0, 1)
            return wide_rows.at[place, :, lanes_of(piece)]
        return slim_rows.at[q, :, pl.ds(OFFSET[piece] - OFFSET[2], WIDTH[piece])]

    def passing(way, q, piece):
        ref = whole_ref(q, piece)
        sent = send_sem.at[GROUPS.index((way, piece, WHOLE))]
        return remote(ref, ref, sent, recv_sem.at[q, piece], target[way])

    def passing_rows(way, q, piece):
        return remote(
            rows_ref(q, piece), held.at[q, pl.ds(0, BOTH), lanes_of(piece)],
            send_sem.at[GROUPS.index((way, piece, ROWS))], recv_sem.at[q, piece], target[way],
        )

    def chosen_rows(q, of):
        group = pl.ds(pl.multiple_of(lax.div(of * CORES, RANK_ROWS) * TOK, TOK), TOK)
        table = ranks_of[q, :, group].astype(F32)
        line = lax.broadcasted_iota(jnp.int32, (RANK_ROWS, TOK), 0)
        slot = lax.broadcasted_iota(jnp.int32, (MOST, TOK), 0).astype(F32)
        first = lax.rem(of * CORES, RANK_ROWS)
        hits = []
        for e in range(CORES):
            rank = jnp.sum(jnp.where(line == first + e, table, 0.0), axis=0, keepdims=True)
            hits.append(slot == rank)
        return hits

    neighbours = (chip + 1, chip - 1, right * Z + z, left * Z + z)

    def pass_on(q, piece):
        whole, some = goes(piece, x, z, lax.div(q, Z), lax.rem(q, Z))
        for way in range(4):
            if (way, piece, WHOLE) in GROUPS:

                @pl.when(whole[way])
                def _(way=way):
                    passing(way, q, piece).start()

        if piece == RANKS:
            return
        of, any_rows = chip, z < 0
        for way in range(4):
            of = jnp.where(some[way], neighbours[way], of)
            any_rows = any_rows | some[way]

        @pl.when(any_rows)
        def _():
            pick = jnp.concatenate([hit.astype(F32) for hit in chosen_rows(q, of)], axis=0)
            rows = jnp.dot(
                pick.astype(BF16), held[q, :, lanes_of(piece)], preferred_element_type=F32
            )
            rows_ref(q, piece)[...] = rows.astype(BF16)
            for way in range(4):
                if (way, piece, ROWS) in GROUPS:

                    @pl.when(some[way])
                    def _(way=way):
                        passing_rows(way, q, piece).start()

    rows = pl.ds(pl.multiple_of(core * RANK_ROWS, RANK_ROWS), RANK_ROWS)

    def quarter(xx):
        return pl.ds(pl.multiple_of(xx * QUARTER, 128), QUARTER)

    router_down = remote(
        r_hbm.at[rows, quarter(x)], rn.at[rows, quarter(x)], r_send.at[0], r_recv.at[0], (below, me)
    )

    @pl.when(s > 0)
    def _():
        router_down.start()

    pass_on(chip, RANKS)
    loads[0].wait()
    for piece in (2, 1, 0, 3):
        pass_on(chip, piece)
    picked_down = remote(picked_v, pk, pk_send, pk_recv, (below, me))
    ids_down = remote(ids_v, next_ids, ids_send, ids_recv, (below, me))

    @pl.when(s > 0)
    def _():
        picked_down.start()
        ids_down.start()

    steps = [by_row(z, words) for words in zip(*map(packed, STEPS))]
    early = [by_row(z, words) for words in zip(*(packed(row[:EARLY]) for row in ORDER))]

    def outputs(which, half, store):
        lhs = hbuf[which].reshape(CHIPS * MOST, FFW)

        @pl.loop(0, HALF // 256)
        def _(t):
            cols = pl.ds(pl.multiple_of(half * HALF + t * 256, 256), 256)
            out = jnp.dot(lhs, wbuf[:, cols], preferred_element_type=F32)
            store(cols, out.astype(BF16).reshape(CHIPS, MOST, 256))

    def store_cross(cols, value):
        cross[:, :, cols] = value

    def store_own(cols, value):
        prod[:, core, :, cols] = value

    def crossing(half):
        cols = pl.ds(half * HALF, HALF)
        return remote(
            cross.at[:, :, cols], prod.at[:, core, :, cols],
            cross_send.at[half], cross_recv.at[half], sibling,
        )

    loads[3].wait()
    for half in range(2):
        loads[4 + half].wait()
        outputs(0, half, store_cross)
        crossing(half).start()
    loads[6].wait()
    for half in range(2):
        outputs(1, half, store_own)

    def arrived(q, piece, ref):
        remote(ref, ref, send_sem.at[0], recv_sem.at[q, piece], target[RIGHT]).wait_recv()

    def take(q, piece):
        if piece == RANKS:
            arrived(q, piece, ranks_of.at[q])
        else:
            full = arrives_whole(piece, x, z, lax.div(q, Z), lax.rem(q, Z))

            @pl.when(full)
            def _():
                arrived(q, piece, held.at[q, :, lanes_of(piece)])

            @pl.when(jnp.logical_not(full))
            def _():
                arrived(q, piece, held.at[q, pl.ds(0, BOTH), lanes_of(piece)])

        pass_on(q, piece)

    def decode(code):
        shard = lax.rem(code, 128)
        xo = lax.rem(x + lax.div(shard, 32), X)
        zo = lax.rem(lax.div(shard, 8), Z)
        return xo * Z + zo, lax.rem(shard, 8)

    def by_piece(piece, act):
        for k in range(5):

            @pl.when(piece == k)
            def _(k=k):
                act(k)

    @pl.loop(0, EARLY)
    def _(i):
        q, piece = decode(entry(early, i))
        by_piece(piece, functools.partial(take, q))

    def spread(k, device):
        ref = rn.at[rows, quarter(x)]
        return remote(ref, ref, r_send.at[1 + k], r_recv.at[1 + k], device)

    def came(k, xx):
        ref = rn.at[rows, quarter(xx)]
        return remote(ref, ref, r_send.at[1 + k], r_recv.at[1 + k], target[2])

    spreads = [spread(0, target[2]), spread(1, target[3]), spread(2, opposite)]
    own_rows = remote(rn.at[rows], rn.at[rows], r_send.at[4], r_recv.at[4], sibling)
    other = pl.ds(pl.multiple_of((1 - core) * RANK_ROWS, RANK_ROWS), RANK_ROWS)
    other_rows = remote(rn.at[other], rn.at[other], r_send.at[4], r_recv.at[4], sibling)

    for half in range(2):
        crossing(half).wait_recv()
    acc[...] = jnp.zeros_like(acc)
    slot_acc[...] = jnp.zeros_like(slot_acc)

    def score_copy(q):
        return remote(
            sent_scores.at[q], st.at[chip], score_send, score_recv,
            (below, q * CORES + core),
        )

    def score(q, piece):
        cols, width = lanes_of(piece), WIDTH[piece]
        full = arrives_whole(piece, x, z, lax.div(q, Z), lax.rem(q, Z))

        @pl.when(full)
        def _():
            acc[q] += lax.dot_general(
                prod[q, :, :, cols].reshape(BOTH, width), held[q, :, cols],
                (((1,), (1,)), ((), ())), preferred_element_type=F32,
            )

        @pl.when(jnp.logical_not(full))
        def _():
            terms = prod[q, :, :, cols].reshape(BOTH, width).astype(F32)
            terms = terms * held[q, :BOTH, cols].astype(F32)
            total = slot_acc[q]
            for k in range(0, width, TOK):
                total = total + terms[:, k : k + TOK]
            slot_acc[q] = total

    def finish(q):
        total = acc[q] + jnp.sum(slot_acc[q], axis=1, keepdims=True)
        lines = []
        for e, hit in enumerate(chosen_rows(q, chip)):
            part = total[e * MOST : (e + 1) * MOST]
            lines.append(jnp.sum(jnp.where(hit, part, 0.0), axis=0, keepdims=True))
        sent_scores[q] = jnp.concatenate(lines, axis=0)

        @pl.when(s > 0)
        def _():
            score_copy(q).start()

    @pl.loop(0, COUNT)
    def _(i):
        code = entry(steps, i)
        q, piece = decode(code)
        new = lax.rem(lax.div(code, 128), 2) == 1

        def step(k):
            @pl.when(new)
            def _():
                take(q, k)

            if k != RANKS:
                score(q, k)

        by_piece(piece, step)

        @pl.when(code >= 256)
        def _():
            finish(q)

        @pl.when((i == COUNT // 4) & (s < sections - 1))
        def _():
            router_down.wait_recv()
            for copy in spreads:
                copy.start()

        @pl.when((i == 3 * COUNT // 4) & (s < sections - 1))
        def _():
            came(0, left).wait_recv()
            came(1, right).wait_recv()
            came(2, across).wait_recv()
            own_rows.start()

    @pl.when(s < sections - 1)
    def _():
        other_rows.wait_recv()
        rn_out[...] = rn[...]
        picked_down.wait_recv()
        ids_down.wait_recv()
        picked = jnp.zeros((EXPERTS, TOK), F32)
        for k in range(ids.shape[0]):
            picked = picked + jnp.where(next_ids[k : k + 1, :] == experts, pk[k : k + 1, :], 0.0)
        weight = picked / jnp.sum(picked, axis=0, keepdims=True)
        slope = weight * (1.0 - picked)
        remote(sent_scores, st, score_send, score_recv, (below, me)).wait_recv()
        score_grad = jnp.concatenate([st[q] for q in range(CHIPS)], axis=0)
        mean_grad = jnp.sum(weight * score_grad, axis=0, keepdims=True)
        table = (score_grad - mean_grad) * slope
        square = jnp.concatenate([table, jnp.zeros((TOK - EXPERTS, TOK), F32)], axis=0)
        table_out[...] = square.T[:, :EXPERTS].astype(BF16)

    @pl.when(s == sections - 1)
    def _():
        rn_out[...] = jnp.zeros_like(rn_out)
        table_out[...] = jnp.zeros_like(table_out)

    for half in range(2):
        crossing(half).wait_send()

    @pl.when(s < sections - 1)
    def _():
        for copy in spreads:
            copy.wait_send()
        own_rows.wait_send()

    @pl.when(s > 0)
    def _():
        router_down.wait_send()
        picked_down.wait_send()
        ids_down.wait_send()
        remote(sent_scores, st, score_send, score_recv, (below, me)).wait_send()

    for row in range(Z):

        @pl.when(z == row)
        def _(row=row):
            for (way, piece, form), n in SENDS[row].items():
                if piece == RANKS:
                    ref = ranks_of.at[pl.ds(0, n)]
                else:
                    ref = held.at[pl.ds(0, n), pl.ds(0, (TOK, BOTH)[form]), lanes_of(piece)]
                sent = send_sem.at[GROUPS.index((way, piece, form))]
                remote(ref, ref, sent, recv_sem.at[0, 0], target[RIGHT]).wait_send()


def exchange(g, ids, logits, h, w, r):
    vmem = pl.BlockSpec(memory_space=pltpu.VMEM)
    dma = pltpu.SemaphoreType.DMA
    return pl.pallas_call(
        kernel,
        out_shape=(
            jax.ShapeDtypeStruct((TOK, EXPERTS), BF16),
            jax.ShapeDtypeStruct((EXPERTS, D), BF16),
        ),
        in_specs=[pl.BlockSpec(memory_space=pl.ANY)] * 6,
        out_specs=(vmem,) * 2,
        scratch_shapes=[
            pltpu.VMEM((CHIPS, TOK, D), BF16),
            pltpu.VMEM((CHIPS, RANK_ROWS, RANK_LANES), BF16),
            pltpu.VMEM((2 * Z, BOTH, OFFSET[2]), BF16),
            pltpu.VMEM((CHIPS, BOTH, D - OFFSET[2]), BF16),
            pltpu.VMEM((CHIPS, CORES, MOST, D), BF16),
            pltpu.VMEM((CHIPS, MOST, D), BF16),
            pltpu.VMEM((CORES, CHIPS, MOST, FFW), BF16),
            pltpu.VMEM((FFW, D), BF16),
            pltpu.VMEM((CHIPS, BOTH, TOK), F32),
            pltpu.VMEM((CHIPS, BOTH, TOK), F32),
            pltpu.VMEM((CHIPS, CORES, TOK), F32),
            pltpu.VMEM(ids.shape, jnp.int32),
            pltpu.VMEM(logits.shape, F32),
            pltpu.VMEM(ids.shape, F32),
            pltpu.VMEM((CHIPS, CORES, TOK), F32),
            pltpu.VMEM((EXPERTS, D), BF16),
            pltpu.VMEM(ids.shape, F32),
            pltpu.VMEM(ids.shape, jnp.int32),
            dma((7,)),
            dma((len(GROUPS),)),
            dma((CHIPS, 5)),
            dma((2,)),
            dma((2,)),
            dma,
            dma,
            dma((5,)),
            dma((5,)),
            dma,
            dma,
            dma,
            dma,
        ],
        compiler_params=pltpu.CompilerParams(
            collective_id=0, has_side_effects=True, vmem_limit_bytes=52 * 2**20
        ),
    )(*(pltpu.with_memory_space_constraint(v, pltpu.HBM) for v in (g, ids, logits, h, w, r)))


def on_device(out_grads, expert_ids, router_logits, hidden_acts, w_down, w_router):
    h = hidden_acts.reshape(CHIPS, CORES, MOST, FFW)
    table, router = exchange(
        out_grads[0], expert_ids[0].T, router_logits[0].T, h, w_down[0, 0], w_router[0]
    )
    return jnp.dot(table, router, preferred_element_type=F32).astype(BF16)[None]


def solution(mesh):
    in_specs = (
        P("pp", "ep", None),
        P("pp", "ep", None),
        P("pp", "ep", None),
        P("pp", "ep", None, None),
        P("pp", "ep", None, None),
        P("pp", None, None),
    )
    out_specs = P("pp", "ep", None)
    return jax.shard_map(
        on_device, mesh=mesh, in_specs=in_specs, out_specs=out_specs, check_vma=False
    )
```
